512 devices in a mesh: leaf: 128 (over z, y, core), near: 4 (over x).
Axes of the slice: x: 4, y: 8, z: 8, core: 2. Of those that a mesh axis runs over, the one named last changes fastest.
Arguments:
- positions: float32 [3, 3072, 512], P(None, 'leaf', 'near'), may hold values from 0 to 1
- noise_variance: float32 [3072, 512], P('leaf', 'near'), may hold values from 0.5 to 2
- solution: float32 [3072, 512], P('leaf', 'near'), may hold values from -6 to 6
- residual: float32 [3072, 512], P('leaf', 'near'), may hold values from -6 to 6
- direction: float32 [3072, 512], P('leaf', 'near'), may hold values from -6 to 6
- leaf_basis: float32 [3072, 64, 512], P('leaf', None, 'near'), may hold values from -0.25 to 0.25
- leaf_skeleton: float32 [3, 3072, 64], P(None, 'leaf'), may hold values from 0 to 1
- leaf_transfer: float32 [3072, 64, 64], P('leaf'), may hold values from -0.75 to 0.75
- box_transfer: float32 [128, 5, 64, 64], P('leaf'), may hold values from -0.75 to 0.75
- box_skeleton: float32 [3, 128, 6, 64], P(None, 'leaf'), may hold values from 0 to 1
- leaf_count: int32 [128], P('leaf'), may hold values from 1 to 24, as said below
- near_list: int32 [3072, 9], P('leaf'), may hold values from -1 to 71, as said below
- far_list: int32 [3072, 8], P('leaf', 'near'), may hold values from -1 to 71, as said below
Outputs:
- new_solution: float32 [3072, 512], P('leaf', 'near')
- new_residual: float32 [3072, 512], P('leaf', 'near')
- new_direction: float32 [3072, 512], P('leaf', 'near')
The draws below stay inside these ranges and needn't reach their ends.
Inputs may be any that keep to these rules, and one draw needn't show every extreme that they name: `leaf_count`: at least one leaf group holds 24 leaves and at least one holds 1, in every draw; a few groups are full, and the others hold up to two thirds of 24. `near_list`: entry 0 is the slot itself; the other entries name distinct occupied slots of the window, or are -1. Slots outside the mesh's first and last groups are never named. `far_list`: entries name distinct occupied slots of the window that are not in the slot's near list, or are -1.
All inputs are finite; a program needn't handle non-finite values.
Results may differ from the reference program's by a relative error of at most 0.0003.
Values sent between devices are 32-bit elements; how exact they have to be, the bound alone decides.
A program may use at most 64 MiB of HBM per device.

```python
import math
import jax
import jax.numpy as jnp
from jax import lax

LEAF_PTS = 512
RANK = 64
LEAF_CAP = 24
NEAR_NB = 9
FAR_NB = 8
GROUPS = 128
SLOTS = 3072
LEVELS = 6


BOX_SIDE = 0.0625


def leaf_centres(slots):
    bit_count = max(2, (SLOTS - 1).bit_length())
    across = jnp.zeros(slots.shape, jnp.int32)
    upward = jnp.zeros(slots.shape, jnp.int32)
    for place in range(bit_count):
        digit = slots // 2 ** place % 2
        if place % 2 == 0:
            across = across + digit * 2 ** (place // 2)
        else:
            upward = upward + digit * 2 ** (place // 2)
    across_cells = 2 ** ((bit_count + 1) // 2)
    upward_cells = 2 ** (bit_count // 2)
    half_side = 0.5 * BOX_SIDE
    centre_x = jnp.clip((across.astype(jnp.float32) + 0.5) / across_cells, half_side, 1.0 - half_side)
    centre_y = jnp.clip((upward.astype(jnp.float32) + 0.5) / upward_cells, half_side, 1.0 - half_side)
    return (centre_x, centre_y)


def inside_boxes(key, slots):
    centre_x, centre_y = leaf_centres(slots)
    unit = jax.random.uniform(key, (3,) + slots.shape, jnp.float32)
    point_x = centre_x + (unit[0] - 0.5) * BOX_SIDE
    point_y = centre_y + (unit[1] - 0.5) * BOX_SIDE
    return jnp.clip(jnp.stack([point_x, point_y, unit[2]], axis=0), 0.0, 1.0)


def draw_positions(key, part):
    key = jax.random.fold_in(key, 201)
    slots = jnp.broadcast_to(jnp.arange(SLOTS, dtype=jnp.int32)[:, None], (SLOTS, LEAF_PTS))
    return inside_boxes(key, slots)


def draw_leaf_skeleton(key, part):
    key = jax.random.fold_in(key, 202)
    slots = jnp.broadcast_to(jnp.arange(SLOTS, dtype=jnp.int32)[:, None], (SLOTS, RANK))
    return inside_boxes(key, slots)


def draw_box_skeleton(key, part):
    key = jax.random.fold_in(key, 203)
    pick_key = jax.random.fold_in(key, 204)
    groups = SLOTS // LEAF_CAP
    first = jnp.arange(groups, dtype=jnp.int32)[:, None] * LEAF_CAP
    widths = (2 ** jnp.arange(LEVELS, dtype=jnp.int32))[None, :] * LEAF_CAP
    lowest = jnp.broadcast_to(first[:, :, None], (groups, LEVELS, RANK))
    highest = jnp.broadcast_to(jnp.minimum(first + widths, SLOTS)[:, :, None], (groups, LEVELS, RANK))
    slots = jax.random.randint(pick_key, (groups, LEVELS, RANK), lowest, highest, dtype=jnp.int32)
    return inside_boxes(key, slots)


def draw_layout(key):
    count_key = jax.random.fold_in(key, 101)
    order_key = jax.random.fold_in(key, 102)
    near_key = jax.random.fold_in(key, 103)
    far_key = jax.random.fold_in(key, 104)
    groups = SLOTS // LEAF_CAP
    counts = jax.random.randint(count_key, (groups,), 1, 2 * LEAF_CAP // 3 + 1, dtype=jnp.int32)
    shuffled = 1 + jax.random.permutation(order_key, groups - 1)
    busiest = max(1, groups // 16)
    counts = counts.at[shuffled[:busiest]].set(LEAF_CAP)
    counts = counts.at[shuffled[busiest]].set(1)
    padded = jnp.concatenate([jnp.zeros((1,), jnp.int32), counts, jnp.zeros((1,), jnp.int32)])
    within = jnp.arange(LEAF_CAP, dtype=jnp.int32)
    occupied = jnp.concatenate([within[None, :] < padded[:-2, None], within[None, :] < counts[:, None], within[None, :] < padded[2:, None]], axis=1)
    occupied = jnp.repeat(occupied, LEAF_CAP, axis=0)
    columns = jnp.arange(3 * LEAF_CAP, dtype=jnp.int32)
    slot_ids = jnp.arange(SLOTS, dtype=jnp.int32)
    itself = LEAF_CAP + slot_ids % LEAF_CAP
    is_self = columns[None, :] == itself[:, None]
    top_column = jnp.max(jnp.where(occupied, columns[None, :], -1), axis=1)
    is_top = columns[None, :] == top_column[:, None]
    even_slot = (slot_ids % 2 == 0)[:, None]
    scores = jax.random.randint(near_key, (SLOTS, 3 * LEAF_CAP), 0, 1 << 17, dtype=jnp.int32) * 1024 + columns[None, :]
    scores = scores + jnp.where(is_top & even_slot, 1 << 28, 0).astype(jnp.int32)
    allowed = occupied & ~is_self & ~(is_top & ~even_slot)
    scores = jnp.where(allowed, scores, -1)
    chosen, picked = lax.top_k(scores, NEAR_NB - 1)
    near_list = jnp.concatenate([itself[:, None], jnp.where(chosen >= 0, picked, -1)], axis=1).astype(jnp.int32)
    listed = jnp.any(columns[None, None, :] == near_list[:, :, None], axis=1)
    far_scores = jax.random.randint(far_key, (SLOTS, 3 * LEAF_CAP), 0, 1 << 17, dtype=jnp.int32) * 1024 + columns[None, :]
    far_scores = far_scores + jnp.where(is_top, 1 << 28, 0).astype(jnp.int32)
    far_scores = jnp.where(occupied & ~listed, far_scores, -1)
    chosen_far, picked_far = lax.top_k(far_scores, FAR_NB)
    far_list = jnp.where(chosen_far >= 0, picked_far, -1).astype(jnp.int32)
    return (counts, near_list, far_list)


def draw_leaf_count(key, part):
    return draw_layout(key)[0]


def draw_near_list(key, part):
    return draw_layout(key)[1]


def draw_far_list(key, part):
    return draw_layout(key)[2]


def shard_levels(own_key, extent, shards, low, top_value):
    def one(axis_at, shards_of):
        draws = jax.random.uniform(jax.random.fold_in(jax.random.fold_in(own_key, 6), axis_at), (shards_of,), jnp.float32, low / len(shards), top_value / len(shards))
        return jnp.repeat(jnp.exp(draws), extent[axis_at] // shards_of).reshape((-1,) + (1,) * (len(extent) - axis_at - 1))

    level = one(*shards[0])
    for cut in shards[1:]:
        level = level * one(*cut)
    return level


def bell_draw(key, dims, spread, limit, shards=(), kind=jnp.bfloat16):
    gain = shard_levels(key, dims, shards, -0.22, 0.18) if shards else 1.0
    array = jax.random.normal(key, dims, jnp.float32) * spread * gain
    return jnp.minimum(jnp.maximum(array, -limit), limit).astype(kind)


def setup_inputs(seed: int = 0) -> dict:
    streams_of = jax.random.split(jax.random.key(seed), 14)
    positions = draw_positions(jax.random.fold_in(streams_of[13], 71), 0)
    noise_variance = jnp.clip(jnp.exp(math.log(2.0) - 1.3862944 * jax.random.uniform(streams_of[1], (SLOTS, LEAF_PTS), jnp.float32) ** shard_levels(streams_of[1], (SLOTS, LEAF_PTS), ((0, 128), (1, 4)), -0.2, 0.2)), 0.5, 2.0)
    solution = bell_draw(streams_of[2], (SLOTS, LEAF_PTS), 1.0, 6.0, ((0, 128), (1, 4)), jnp.float32)
    residual = bell_draw(streams_of[3], (SLOTS, LEAF_PTS), 1.0, 6.0, ((0, 128), (1, 4)), jnp.float32)
    direction = bell_draw(streams_of[4], (SLOTS, LEAF_PTS), 1.0, 6.0, ((0, 128), (1, 4)), jnp.float32)
    leaf_basis = bell_draw(streams_of[5], (SLOTS, RANK, LEAF_PTS), LEAF_PTS ** -0.5, 0.25, ((0, 128), (2, 4)), jnp.float32)
    leaf_skeleton = draw_leaf_skeleton(jax.random.fold_in(streams_of[13], 71), 0)
    leaf_transfer = bell_draw(streams_of[7], (SLOTS, RANK, RANK), RANK ** -0.5, 0.75, ((0, 128),), jnp.float32)
    box_transfer = bell_draw(streams_of[8], (GROUPS, LEVELS - 1, RANK, RANK), RANK ** -0.5, 0.75, ((0, 128),), jnp.float32)
    box_skeleton = draw_box_skeleton(jax.random.fold_in(streams_of[13], 71), 0)
    leaf_count = draw_leaf_count(jax.random.fold_in(streams_of[13], 71), 0)
    near_list = draw_near_list(jax.random.fold_in(streams_of[13], 71), 0)
    far_list = draw_far_list(jax.random.fold_in(streams_of[13], 71), 0)
    return {"positions": positions, "noise_variance": noise_variance, "solution": solution, "residual": residual, "direction": direction, "leaf_basis": leaf_basis, "leaf_skeleton": leaf_skeleton, "leaf_transfer": leaf_transfer, "box_transfer": box_transfer, "box_skeleton": box_skeleton, "leaf_count": leaf_count, "near_list": near_list, "far_list": far_list}


AMPLITUDE = 0.02
LENGTH = 0.5
HIGHEST = lax.Precision.HIGHEST

def kernel_block(targets, sources):
    squared = None
    for component in range(3):
        spacing = targets[component][..., :, None] - sources[component][..., None, :]
        squared = spacing * spacing if squared is None else squared + spacing * spacing
    return AMPLITUDE * jnp.exp(-jnp.sqrt(squared) / LENGTH)

def reference(positions, noise_variance, solution, residual, direction, leaf_basis, leaf_skeleton, leaf_transfer, box_transfer, box_skeleton, leaf_count, near_list, far_list):
    slot_ids = jnp.arange(SLOTS, dtype=jnp.int32)
    device = slot_ids // LEAF_CAP
    occupied = (slot_ids % LEAF_CAP < leaf_count[device])[:, None]
    masked_direction = jnp.where(occupied, direction, 0.0)
    masked_residual = jnp.where(occupied, residual, 0.0)
    masked_solution = jnp.where(occupied, solution, 0.0)
    window_base = device * LEAF_CAP - LEAF_CAP
    near_present = near_list >= 0
    near_global = jnp.where(near_present, window_base[:, None] + near_list, 0).astype(jnp.int32)

    def near_one(items):
        targets, indices, present = items
        sources = positions[:, indices, :].reshape(3, NEAR_NB * LEAF_PTS)
        weights = (masked_direction[indices] * present[:, None]).reshape(NEAR_NB * LEAF_PTS)
        kernel_tile = kernel_block(targets, sources)
        return lax.optimization_barrier(jnp.sum(kernel_tile * weights[None, :], axis=1))
    near_term = lax.map(near_one, (positions.transpose(1, 0, 2), near_global, near_present))
    coeffs = jnp.einsum('srp,sp->sr', leaf_basis, masked_direction, precision=HIGHEST)
    far_present = far_list >= 0
    far_global = jnp.where(far_present, window_base[:, None] + far_list, 0).astype(jnp.int32)

    def far_one(items):
        skeleton, indices, present = items
        sources = leaf_skeleton[:, indices, :]
        weights = coeffs[indices] * present[:, None]
        kernel_tile = kernel_block(skeleton[:, None, :], sources)
        return jnp.einsum('fxy,fy->x', kernel_tile, weights, precision=HIGHEST)
    far_local = lax.map(far_one, (leaf_skeleton.transpose(1, 0, 2), far_global, far_present))
    content = jnp.einsum('dsab,dsb->da', leaf_transfer.reshape(GROUPS, LEAF_CAP, RANK, RANK), coeffs.reshape(GROUPS, LEAF_CAP, RANK), precision=HIGHEST)
    ascending = [content]
    for height in range(LEVELS - 1):
        stride = 2 ** height
        transfer = box_transfer[::stride, height]
        lifted = jnp.einsum('bxy,by->bx', transfer, ascending[-1], precision=HIGHEST)
        ascending.append(lifted[0::2] + lifted[1::2])
    local_fields = []
    for height in range(LEVELS):
        stride = 2 ** height
        box_count = GROUPS // stride
        skeleton = box_skeleton[:, ::stride, height, :]
        parity = jnp.arange(box_count, dtype=jnp.int32) % 2
        padded_content = jnp.pad(ascending[height], ((3, 3), (0, 0)))
        padded_skeleton = jnp.pad(skeleton, ((0, 0), (3, 3), (0, 0)))
        field = jnp.zeros_like(ascending[height])
        for offset in (-3, -2, 2, 3):
            other = padded_content[3 + offset:3 + offset + box_count]
            other_skeleton = padded_skeleton[:, 3 + offset:3 + offset + box_count]
            kernel_tile = kernel_block(skeleton, other_skeleton)
            contribution = jnp.einsum('bxy,by->bx', kernel_tile, other, precision=HIGHEST)
            if offset == -3:
                contribution = jnp.where((parity == 1)[:, None], contribution, 0.0)
            elif offset == 3:
                contribution = jnp.where((parity == 0)[:, None], contribution, 0.0)
            field = field + contribution
        local_fields.append(field)
    downward = local_fields[LEVELS - 1]
    for height in range(LEVELS - 2, -1, -1):
        stride = 2 ** height
        transfer = box_transfer[::stride, height]
        parent = jnp.repeat(downward, 2, axis=0)
        downward = local_fields[height] + jnp.einsum('byx,by->bx', transfer, parent, precision=HIGHEST)
    expansion = far_local + jnp.einsum('sba,sb->sa', leaf_transfer, downward[device], precision=HIGHEST)
    far_values = jnp.einsum('srp,sr->sp', leaf_basis, expansion, precision=HIGHEST)
    image = jnp.where(occupied, noise_variance * masked_direction + near_term + far_values, 0.0)
    norm_old = jnp.sum(masked_residual * masked_residual)
    curvature = jnp.sum(masked_direction * image)
    step_length = norm_old / curvature
    new_solution = masked_solution + step_length * masked_direction
    new_residual = masked_residual - step_length * image
    norm_new = jnp.sum(new_residual * new_residual)
    new_direction = new_residual + norm_new / norm_old * masked_direction
    return (new_solution, new_residual, new_direction)
```

```python
import functools

import jax
import jax.numpy as jnp
from jax import lax
from jax.experimental import pallas as pl
from jax.experimental.pallas import tpu as pltpu
from jax.sharding import PartitionSpec as P

AMPLITUDE = 0.02
SCALE = 2.0 * 1.4426950408889634
HIGHEST = lax.Precision.HIGHEST
MESH = pl.DeviceIdType.MESH
F32 = jnp.float32
BF16 = jnp.bfloat16
CAP = 24
NEAR = 4
PLANE = 16
PLANES = 8
NEAR_NB = 9
LEVELS = 6
SPLIT_ROWS = 48
TINY = 1e-12


def pieces(tile):
    high = tile.astype(BF16).astype(F32)
    rest = tile - high
    middle = rest.astype(BF16).astype(F32)
    return high, middle, rest - middle


def decay(squared):
    clamped = jnp.maximum(squared, TINY)
    return jnp.exp2(-(clamped * lax.rsqrt(clamped)))


def row_times(row, matrix, transposed):
    dims = (((1,), (1 if transposed else 0,)), ((), ()))
    wide = jnp.broadcast_to(row, (8, row.shape[1]))
    return lax.dot_general(
        wide, matrix, dims, precision=HIGHEST, preferred_element_type=F32
    )[0:1]


def padded_square(block):
    rows, lanes = block.shape
    if lanes < 128:
        block = jnp.concatenate([block, jnp.zeros((rows, 128 - lanes), F32)], axis=1)
    if rows < 128:
        block = jnp.concatenate([block, jnp.zeros((128 - rows, 128), F32)], axis=0)
    return block


def kernel(
    count_ref, near_ref, far_ref,
    pos_ref, noise_ref, sol_ref, res_ref, dir_ref, basis_ref, lskel_ref, ltrans_ref,
    btrans_ref, bskel_ref,
    new_sol_ref, new_res_ref, new_dir_ref,
    win0, win1, win2, win3, split0, split3, wb0, wb3, tsplit, products0, products3, acc, near_rows,
    cbuf, fbuf, farwin, ftarget, pbuf, bufa, big, small, far_rows, ebuf, far_vals, targets,
    hop1, hop2, hop3,
    win_s, win_r, c_s, c_r, l_s, l_r, p_s, p_r, relay_s, relay_r, a_s, a_r, b_s, b_r, g_s, g_r,
    f_s, f_r, h1_s, h1_r, h2_s, h2_r, h3_s, h3_r,
):
    leaf = lax.axis_index("leaf")
    near = lax.axis_index("near")
    plane = leaf // PLANE
    place = lax.rem(leaf, PLANE)
    across = place // 2
    core = lax.rem(place, 2)
    wins = (win0, win1, win2, win3)

    def to(leaf_at, near_at):
        return {"leaf": leaf_at, "near": near_at}

    def send_to(src, dst, send_sem, recv_sem, leaf_at, near_at):
        return pltpu.make_async_remote_copy(
            src_ref=src, dst_ref=dst, send_sem=send_sem, recv_sem=recv_sem,
            device_id=to(leaf_at, near_at), device_id_type=MESH,
        )

    def near_at(step):
        return lax.rem(near + step, NEAR)

    def leaf_at(step):
        return lax.rem(leaf + step + PLANE * PLANES, PLANE * PLANES)

    def plane_peer(step):
        return plane * PLANE + lax.rem(place + step, PLANE)

    def depth_peer(step):
        return lax.rem(plane + step + PLANES, PLANES) * PLANE + place

    barrier = pltpu.get_barrier_semaphore()

    def greet(leaf_to, near_to):
        pl.semaphore_signal(barrier, inc=1, device_id=to(leaf_to, near_to), device_id_type=MESH)

    for step in range(1, NEAR):
        greet(leaf, near_at(step))
    for way in (1, -1):
        for step in range(NEAR):
            greet(leaf_at(way), near_at(step))

    @pl.loop(1, PLANE)
    def _(step):
        greet(plane_peer(step), near)

    @pl.loop(1, PLANES)
    def _(step):
        greet(depth_peer(step), near)

    count = count_ref[0]
    occupied = lax.broadcasted_iota(jnp.int32, (CAP, 128), 0) < count
    direction = jnp.where(occupied, dir_ref[...], 0.0)
    for component in range(3):
        win0[pl.ds(96 + component, CAP, stride=4), :] = pos_ref[component] * SCALE
    win0[pl.ds(99, CAP, stride=4), :] = direction

    pl.semaphore_wait(barrier, 3 + 8 + PLANE - 1 + PLANES - 1)

    own = win0.at[pl.ds(96, 96), :]
    window_copies = {}
    number = 0
    for way, group in ((1, 0), (-1, 2), (0, 1)):
        for step in range(NEAR):
            if way == 0 and step == 0:
                continue
            chunk = (NEAR - step) % NEAR
            window_copies[way, step] = send_to(
                own, wins[chunk].at[pl.ds(96 * group, 96), :], win_s.at[number], win_r.at[number],
                leaf_at(way), near_at(step),
            )
            number += 1
    for way in (1, -1):
        window_copies[way, 0].start()

    pair_copies = []
    for level, first in ((2, 0), (3, 1), (4, 4)):
        span = 2 ** (level - 1)
        for step in range(1, span):
            pair_copies.append((span, send_to(
                btrans_ref.at[0, level], pbuf.at[level - 1], p_s.at[first + step - 1], p_r.at[level - 2],
                leaf_at(2 * step), near,
            )))
    relay = send_to(pbuf, pbuf, relay_s, relay_r, leaf_at(1), near)

    @pl.when(core == 0)
    def _():
        pbuf[0] = btrans_ref[0, 1]
        for level in (2, 3, 4):
            @pl.when(lax.rem(across, 2 ** (level - 1)) == 0)
            def _(level=level):
                pbuf[level - 1] = btrans_ref[0, level]
                for span, copy in pair_copies:
                    if span == 2 ** (level - 1):
                        copy.start()

    lanes64 = lax.broadcasted_iota(jnp.int32, (64, 128), 1)

    def one_coeff(slot, columns):
        product = basis_ref[slot] * jnp.where(slot < count, dir_ref[pl.ds(slot, 1), :], 0.0)
        return jnp.where(lanes64 == slot, jnp.sum(product, axis=1, keepdims=True), columns)

    columns = lax.fori_loop(0, CAP, one_coeff, jnp.zeros((64, 128), F32), unroll=4)
    cbuf[near] = padded_square(columns).T[0:CAP, 0:64]
    c_copies = []
    for step in range(1, NEAR):
        copy = send_to(cbuf.at[near], cbuf.at[near], c_s.at[step - 1], c_r.at[step - 1], leaf, near_at(step))
        copy.start()
        c_copies.append(copy)
    for way in (0, 1, -1):
        for step in range(1, NEAR):
            window_copies[way, step].start()

    sub = lax.broadcasted_iota(jnp.int32, (8, 128), 0)
    centre = jnp.zeros((8, 128), F32)
    for component in range(3):
        middle = jnp.mean(pos_ref[component]) * SCALE
        centre = jnp.where((sub == component) | (sub == component + 4), middle, centre)

    def extended(tile):
        square = tile * tile
        norm = square[0:1] + square[1:2] + square[2:3]
        return norm

    def prepare_target(pair, carry):
        tile = win0[pl.ds(pl.multiple_of(96 + 8 * pair, 8), 8), :] - centre
        for half in range(2):
            base = tile if half == 0 else pltpu.roll(tile, 4, 0)
            norm = extended(base)
            rows = jnp.where(sub < 3, -2.0 * base, jnp.where(sub == 3, 1.0, jnp.where(sub == 4, norm, 0.0)))
            high, middle, low = pieces(rows)
            stacked = jnp.concatenate(
                [high, high, middle, middle, high, low, jnp.zeros((128 - SPLIT_ROWS, 128), F32)], axis=0
            )
            tsplit[2 * pair + half] = stacked.T[:, 0:SPLIT_ROWS].astype(BF16)
        return carry

    lax.fori_loop(0, CAP // 2, prepare_target, 0)

    def prepare_sources(window, split, weights, at, lanes):
        split[3 * CAP, :, lanes] = jnp.zeros((SPLIT_ROWS, 128), BF16)
        weights[3 * CAP, at] = jnp.zeros((8, 128), F32)

        def one(pair, carry):
            tile = window[pl.ds(pl.multiple_of(8 * pair, 8), 8), :] - centre
            for half in range(2):
                base = tile if half == 0 else pltpu.roll(tile, 4, 0)
                norm = extended(base)
                rows = jnp.where(sub < 3, base, jnp.where(sub == 3, norm, jnp.where(sub == 4, 1.0, 0.0)))
                high, middle, low = pieces(rows)
                stacked = jnp.concatenate([high, middle, high, middle, low, high], axis=0)
                split[2 * pair + half, :, lanes] = stacked.astype(BF16)
                weights[2 * pair + half, at] = jnp.broadcast_to(base[3:4], (8, 128))
            return carry

        lax.fori_loop(0, 3 * CAP // 2, one, 0, unroll=2)

    skeleton_rows = padded_square(
        jnp.concatenate([lskel_ref[0], lskel_ref[1], lskel_ref[2]], axis=0) * SCALE
    ).T
    for row in range(3 * CAP):
        ftarget[row] = jnp.broadcast_to(skeleton_rows[0:64, row:row + 1], (64, 64))
    for component in range(3):
        farwin[component, CAP:2 * CAP, :] = lskel_ref[component] * SCALE
    farwin[:, 3 * CAP:, :] = jnp.zeros((4, 8, 64), F32)

    for copy in c_copies:
        copy.wait_recv()
    coeffs = cbuf[0] + cbuf[1] + cbuf[2] + cbuf[3]
    farwin[3, CAP:2 * CAP, :] = coeffs
    l_copies = []
    for number, (way, group) in enumerate(((1, 0), (-1, 2))):
        copy = send_to(
            farwin.at[:, pl.ds(CAP, CAP), :], farwin.at[:, pl.ds(CAP * group, CAP), :],
            l_s.at[number], l_r.at[number], leaf_at(way), near,
        )
        copy.start()
        l_copies.append(copy)

    for level in (2, 3, 4):
        @pl.when((core == 0) & (lax.rem(across, 2 ** (level - 1)) != 0))
        def _(level=level):
            send_to(
                btrans_ref.at[0, level], pbuf.at[level - 1], p_s.at[0], p_r.at[level - 2], leaf, near
            ).wait_recv()

    @pl.when(core == 0)
    def _():
        relay.start()

    total = jnp.zeros((64, 64), F32)
    for slot in range(CAP):
        total = total + ltrans_ref[slot] * farwin[3, CAP + slot:CAP + slot + 1, :]
    lifted = padded_square(jnp.broadcast_to(jnp.sum(total, axis=1, keepdims=True), (64, 128))).T[0:1, 0:64]

    @pl.when(core == 1)
    def _():
        relay.wait_recv()

    bufa[place] = jnp.zeros((32, 64), F32)
    bufa[place, 0:1, :] = lifted
    for level in range(LEVELS - 1):
        matrix = btrans_ref[0, 0] if level == 0 else pbuf[level - 1]
        lifted = row_times(lifted, matrix, True)
        bufa[place, level + 1:level + 2, :] = lifted
    for component in range(3):
        bufa[place, 8 * (component + 1):8 * (component + 1) + LEVELS, :] = bskel_ref[component, 0] * SCALE

    def a_copy(step):
        return send_to(bufa.at[place], bufa.at[place], a_s.at[step], a_r.at[step], plane_peer(step), near)

    @pl.loop(1, PLANE)
    def _(step):
        a_copy(step).start()

    def near_slots(low, high, split, weights, products, width, first):
        def listed(slot, place_in_list):
            index = near_ref[slot, place_in_list]
            return jnp.where(index < 0, 3 * CAP, index)

        def multiply(slot, index, buffer):
            products[buffer] = jnp.dot(tsplit[slot], split[index], preferred_element_type=F32)

        def one_slot(slot, carry):
            indices = [listed(slot, k) for k in range(NEAR_NB)]
            following = jnp.minimum(slot + 1, CAP - 1)
            if first:
                sums = [jnp.zeros((8, 128), F32)] * 16
            else:
                sums = [acc[slot, 8 * g:8 * g + 8, :] for g in range(16)]
            for k in range(NEAR_NB):
                if k + 1 < NEAR_NB:
                    multiply(slot, indices[k + 1], (k + 1) % 3)
                else:
                    multiply(following, listed(following, 0), 0)
                weight = [weights[indices[k], j] for j in range(width)]
                for g in range(16):
                    for j in range(width):
                        tile = decay(products[k % 3, 8 * g:8 * g + 8, 128 * j:128 * j + 128])
                        sums[g] = sums[g] + tile * weight[j]
            if first:
                for g in range(16):
                    acc[slot, 8 * g:8 * g + 8, :] = sums[g]
            else:
                whole = jnp.concatenate(sums, axis=0).T
                near_rows[pl.ds(slot, 1), :] = jnp.sum(whole, axis=0, keepdims=True)
            return carry

        multiply(low, listed(low, 0), 0)
        lax.fori_loop(low, high, one_slot, 0)

    for way in (1, -1):
        window_copies[way, 0].wait_recv()
    prepare_sources(win0, split0, wb0, 0, slice(0, 128))
    near_slots(0, CAP, split0, wb0, products0, 1, True)

    @pl.loop(1, PLANE)
    def _(step):
        a_copy(step).wait_recv()

    sums = [bufa[i, 0:8, :] for i in range(PLANE)]
    offset = 0
    for level in range(LEVELS):
        span = 2 ** min(level, 4)
        if 0 < level < 5:
            sums = [sums[2 * i] + sums[2 * i + 1] for i in range(len(sums) // 2)]
        for box in range(PLANE // span):
            rows = [sums[box][level:level + 1, :]] + [
                bufa[box * span, 8 * (c + 1) + level:8 * (c + 1) + level + 1, :] for c in range(3)
            ]
            for c in range(4):
                if level < 3:
                    big[1, c, offset + box:offset + box + 1, :] = rows[c]
                else:
                    at = 4 * c + (0, 2, 3)[level - 3] + box
                    small[plane, at:at + 1, :] = rows[c]
        offset += PLANE // span

    def b_copy(step):
        return send_to(small.at[plane], small.at[plane], b_s.at[step], b_r.at[step], depth_peer(step), near)

    @pl.loop(1, PLANES)
    def _(step):
        b_copy(step).start()

    g_copies = []
    for number, (way, slot) in enumerate(((1, 0), (-1, 2))):
        copy = send_to(big.at[1], big.at[slot], g_s.at[number], g_r.at[number], depth_peer(way), near)
        copy.start()
        g_copies.append(copy)

    for way in (1, -1, 0):
        for step in range(1, NEAR):
            window_copies[way, step].wait_recv()
    for j in range(3):
        prepare_sources(wins[j + 1], split3, wb3, j, slice(128 * j, 128 * j + 128))
    near_slots(0, 8, split3, wb3, products3, 3, False)

    for copy in l_copies:
        copy.wait_recv()

    def one_far(slot, carry):
        target = [ftarget[c * CAP + slot] for c in range(3)]
        running = jnp.zeros((64, 64), F32)
        for k in range(2):
            index = far_ref[slot, k]
            index = jnp.where(index < 0, 3 * CAP, index)
            squared = jnp.zeros((64, 64), F32)
            for c in range(3):
                spacing = target[c] - farwin[c, pl.ds(index, 1), :]
                squared = squared + spacing * spacing
            running = running + decay(squared) * farwin[3, pl.ds(index, 1), :]
        return jnp.where(lanes64 == slot, jnp.sum(running, axis=1, keepdims=True), carry)

    far_columns = lax.fori_loop(0, CAP, one_far, jnp.zeros((64, 128), F32), unroll=2)
    fbuf[near] = padded_square(far_columns).T[0:CAP, 0:64] * AMPLITUDE
    f_copies = []
    for step in range(1, NEAR):
        copy = send_to(fbuf.at[near], fbuf.at[near], f_s.at[step - 1], f_r.at[step - 1], leaf, near_at(step))
        copy.start()
        f_copies.append(copy)

    @pl.loop(1, PLANES)
    def _(step):
        b_copy(step).wait_recv()

    for copy in g_copies:
        copy.wait_recv()
    targets[...] = jnp.zeros((128, 128), F32)
    for level in range(LEVELS):
        for c in range(3):
            if level < 5:
                first = place // 2 ** level * 2 ** level
                row = bufa[first, 8 * (c + 1) + level:8 * (c + 1) + level + 1, :]
            else:
                row = small[plane // 2 * 2, 4 * c + 7:4 * c + 8, :]
            targets[3 * level + c:3 * level + c + 1, 0:64] = row
    turned = targets[...].T
    offsets = (0, 16, 24)
    field_columns = jnp.zeros((64, 128), F32)
    for level in range(LEVELS):
        box = leaf // 2 ** level
        boxes = PLANE * PLANES // 2 ** level
        target = [jnp.broadcast_to(turned[0:64, 3 * level + c:3 * level + c + 1], (64, 64)) for c in range(3)]
        running = jnp.zeros((64, 64), F32)
        for away in (jnp.where(lax.rem(box, 2) == 1, -3, 3), -2, 2):
            other = box + away
            exists = (other >= 0) & (other < boxes)
            other = jnp.clip(other, 0, boxes - 1)
            if level < 3:
                each = PLANE // 2 ** level
                other_plane = other // each - plane + 1
                at = offsets[level] + lax.rem(other, each)
                rows = [big[other_plane, c, pl.ds(at, 1), :] for c in range(4)]
            elif level < 5:
                each = PLANE // 2 ** level
                at = (0, 2)[level - 3] + lax.rem(other, each)
                rows = [small[other // each, pl.ds(4 * c + at, 1), :] for c in range(4)]
            else:
                rows = [small[2 * other, 4 * c + 3:4 * c + 4, :] for c in range(4)]
                rows[0] = rows[0] + small[2 * other + 1, 3:4, :]
            squared = jnp.zeros((64, 64), F32)
            for c in range(3):
                spacing = target[c] - rows[c + 1]
                squared = squared + spacing * spacing
            running = running + decay(squared) * jnp.where(exists, rows[0], 0.0)
        field_columns = jnp.where(lanes64 == level, jnp.sum(running, axis=1, keepdims=True), field_columns)
    fields = padded_square(field_columns).T[0:8, 0:64] * AMPLITUDE
    downward = fields[LEVELS - 1:LEVELS]
    for level in range(LEVELS - 2, -1, -1):
        matrix = btrans_ref[0, 0] if level == 0 else pbuf[level - 1]
        downward = fields[level:level + 1] + row_times(downward, matrix, False)
    down_column = jnp.broadcast_to(
        jnp.concatenate([downward, jnp.zeros((1, 64), F32)], axis=1), (128, 128)
    ).T[0:64, 0:64]
    for slot in range(CAP):
        far_rows[slot:slot + 1, :] = jnp.sum(ltrans_ref[slot] * down_column, axis=0, keepdims=True)

    near_slots(8, 16, split3, wb3, products3, 3, False)

    for copy in f_copies:
        copy.wait_recv()
    expansion = far_rows[...] + (fbuf[0] + fbuf[1] + fbuf[2] + fbuf[3])
    expansion_columns = padded_square(expansion).T
    for slot in range(CAP):
        far_vals[slot:slot + 1, :] = jnp.sum(
            basis_ref[slot] * expansion_columns[0:64, slot:slot + 1], axis=0, keepdims=True
        )

    near_slots(16, CAP, split3, wb3, products3, 3, False)

    residual = jnp.where(occupied, res_ref[...], 0.0)
    image = jnp.where(
        occupied, noise_ref[...] * direction + AMPLITUDE * near_rows[...] + far_vals[...], 0.0
    )
    tile = jnp.zeros((8, 128), F32)
    for number, product in enumerate(
        (residual * residual, direction * image, residual * image, image * image)
    ):
        tile = jnp.where(sub == number, jnp.sum(product, axis=0, keepdims=True), tile)

    hop1[near] = tile
    h1_copies = []
    for step in range(1, NEAR):
        copy = send_to(hop1.at[near], hop1.at[near], h1_s.at[step], h1_r.at[step], leaf, near_at(step))
        copy.start()
        h1_copies.append(copy)
    for copy in h1_copies:
        copy.wait_recv()
    tile = hop1[0] + hop1[1] + hop1[2] + hop1[3]

    hop2[place] = tile

    def h2_copy(step):
        return send_to(hop2.at[place], hop2.at[place], h2_s.at[step], h2_r.at[step], plane_peer(step), near)

    @pl.loop(1, PLANE)
    def _(step):
        h2_copy(step).start()

    @pl.loop(1, PLANE)
    def _(step):
        h2_copy(step).wait_recv()

    tile = jnp.sum(hop2[...], axis=0)

    hop3[plane] = tile

    def h3_copy(step):
        return send_to(hop3.at[plane], hop3.at[plane], h3_s.at[step], h3_r.at[step], depth_peer(step), near)

    @pl.loop(1, PLANES)
    def _(step):
        h3_copy(step).start()

    @pl.loop(1, PLANES)
    def _(step):
        h3_copy(step).wait_recv()

    totals = jnp.sum(jnp.sum(hop3[...], axis=0), axis=1, keepdims=True)
    norm_old, curvature, mixed, image_norm = (totals[i:i + 1] for i in range(4))
    step_length = norm_old / curvature
    norm_new = norm_old - 2.0 * step_length * mixed + step_length * step_length * image_norm
    new_residual = residual - step_length * image
    new_sol_ref[...] = jnp.where(occupied, sol_ref[...], 0.0) + step_length * direction
    new_res_ref[...] = new_residual
    new_dir_ref[...] = new_residual + norm_new / norm_old * direction

    for copy in window_copies.values():
        copy.wait_send()

    @pl.when(core == 0)
    def _():
        relay.wait_send()
        for level in (2, 3, 4):
            @pl.when(lax.rem(across, 2 ** (level - 1)) == 0)
            def _(level=level):
                for span, copy in pair_copies:
                    if span == 2 ** (level - 1):
                        copy.wait_send()

    for copy in c_copies + l_copies + g_copies + f_copies + h1_copies:
        copy.wait_send()

    @pl.loop(1, PLANE)
    def _(step):
        a_copy(step).wait_send()
        h2_copy(step).wait_send()

    @pl.loop(1, PLANES)
    def _(step):
        b_copy(step).wait_send()
        h3_copy(step).wait_send()


def per_device(
    positions, noise_variance, solution, residual, direction, leaf_basis, leaf_skeleton,
    leaf_transfer, box_transfer, box_skeleton, leaf_count, near_list, far_list,
):
    vmem = pl.BlockSpec(memory_space=pltpu.VMEM)
    smem = pl.BlockSpec(memory_space=pltpu.SMEM)
    dma = pltpu.SemaphoreType.DMA
    out = jax.ShapeDtypeStruct((CAP, 128), F32)
    slots = 3 * CAP + 1
    return pl.pallas_call(
        kernel,
        out_shape=(out, out, out),
        in_specs=[smem] * 3 + [vmem] * 10,
        out_specs=(vmem, vmem, vmem),
        scratch_shapes=[
            *[pltpu.VMEM((12 * CAP, 128), F32)] * 4,
            pltpu.VMEM((slots, SPLIT_ROWS, 128), BF16),
            pltpu.VMEM((slots, SPLIT_ROWS, 384), BF16),
            pltpu.VMEM((slots, 1, 8, 128), F32),
            pltpu.VMEM((slots, 3, 8, 128), F32),
            pltpu.VMEM((CAP, 128, SPLIT_ROWS), BF16),
            pltpu.VMEM((3, 128, 128), F32),
            pltpu.VMEM((3, 128, 384), F32),
            pltpu.VMEM((CAP, 128, 128), F32),
            pltpu.VMEM((CAP, 128), F32),
            pltpu.VMEM((NEAR, CAP, 64), F32),
            pltpu.VMEM((NEAR, CAP, 64), F32),
            pltpu.VMEM((4, 3 * CAP + 8, 64), F32),
            pltpu.VMEM((3 * CAP, 64, 64), F32),
            pltpu.VMEM((4, 64, 64), F32),
            pltpu.VMEM((PLANE, 32, 64), F32),
            pltpu.VMEM((3, 4, 32, 64), F32),
            pltpu.VMEM((PLANES, 16, 64), F32),
            pltpu.VMEM((CAP, 64), F32),
            pltpu.VMEM((CAP, 64), F32),
            pltpu.VMEM((CAP, 128), F32),
            pltpu.VMEM((128, 128), F32),
            pltpu.VMEM((NEAR, 8, 128), F32),
            pltpu.VMEM((PLANE, 8, 128), F32),
            pltpu.VMEM((PLANES, 8, 128), F32),
            dma((11,)), dma((11,)), dma((3,)), dma((3,)), dma((2,)), dma((2,)),
            dma((11,)), dma((3,)), dma, dma, dma((PLANE,)), dma((PLANE,)),
            dma((PLANES,)), dma((PLANES,)), dma((2,)), dma((2,)),
            dma((3,)), dma((3,)), dma((NEAR,)), dma((NEAR,)),
            dma((PLANE,)), dma((PLANE,)), dma((PLANES,)), dma((PLANES,)),
        ],
        compiler_params=pltpu.CompilerParams(
            collective_id=0, has_side_effects=True, vmem_limit_bytes=48 * 2**20
        ),
        name="iteration",
    )(
        leaf_count, near_list, far_list,
        positions, noise_variance, solution, residual, direction, leaf_basis, leaf_skeleton,
        leaf_transfer, box_transfer, box_skeleton,
    )


def solution(mesh):
    return jax.shard_map(
        per_device,
        mesh=mesh,
        in_specs=(
            P(None, "leaf", "near"),
            P("leaf", "near"),
            P("leaf", "near"),
            P("leaf", "near"),
            P("leaf", "near"),
            P("leaf", None, "near"),
            P(None, "leaf", None),
            P("leaf", None, None),
            P("leaf", None, None, None),
            P(None, "leaf", None, None),
            P("leaf"),
            P("leaf", None),
            P("leaf", "near"),
        ),
        out_specs=(P("leaf", "near"), P("leaf", "near"), P("leaf", "near")),
        check_vma=False,
    )
```

```python
import functools

import jax
import jax.numpy as jnp
from jax import lax
from jax.experimental import pallas as pl
from jax.experimental.pallas import tpu as pltpu
from jax.sharding import PartitionSpec as P

AMPLITUDE = 0.02
SCALE = 2.0 * 1.4426950408889634
HIGHEST = lax.Precision.HIGHEST
MESH = pl.DeviceIdType.MESH
F32 = jnp.float32
BF16 = jnp.bfloat16
CAP = 24
NEAR = 4
PLANE = 16
PLANES = 8
NEAR_NB = 9
LEVELS = 6
SPLIT_ROWS = 48
TINY = 1e-12


def pieces(tile):
    high = tile.astype(BF16).astype(F32)
    rest = tile - high
    middle = rest.astype(BF16).astype(F32)
    return high, middle, rest - middle


def decay(squared):
    clamped = jnp.maximum(squared, TINY)
    return jnp.exp2(-(clamped * lax.rsqrt(clamped)))


def row_times(row, matrix, transposed):
    dims = (((1,), (1 if transposed else 0,)), ((), ()))
    wide = jnp.broadcast_to(row, (8, row.shape[1]))
    return lax.dot_general(
        wide, matrix, dims, precision=HIGHEST, preferred_element_type=F32
    )[0:1]


def padded_square(block):
    rows, lanes = block.shape
    if lanes < 128:
        block = jnp.concatenate([block, jnp.zeros((rows, 128 - lanes), F32)], axis=1)
    if rows < 128:
        block = jnp.concatenate([block, jnp.zeros((128 - rows, 128), F32)], axis=0)
    return block


def kernel(
    count_ref, near_ref, far_ref,
    pos_in, noise_in, sol_in, res_in, dir_in, basis_in, lskel_in, ltrans_in, btrans_in, bskel_in,
    kept_sol_ref, kept_res_ref, res_step_ref, kept_dir_ref, step_ref, ratio_ref,
    pos_ref, noise_ref, sol_ref, res_ref, dir_ref, basis_ref, lskel_ref, ltrans_ref, btrans_ref, bskel_ref, in_sem,
    win0, win1, win2, win3, split0, split3, wb0, wb3, tsplit, products, acc, near_rows,
    cbuf, fbuf, farwin, ftarget, psend, pbuf, bufa, big, small, far_rows, ebuf, far_vals, targets,
    hop1, hop2,
    win_s, win_r, c_s, c_r, l_s, l_r, p_s, p_r, relay_s, relay_r, a_s, a_r, b_s, b_r, g_s, g_r,
    f_s, f_r, h1_s, h1_r, h2_s, h2_r,
):
    leaf = lax.axis_index("leaf")
    near = lax.axis_index("near")
    plane = leaf // PLANE
    place = lax.rem(leaf, PLANE)
    across = place // 2
    core = lax.rem(place, 2)
    wins = (win0, win1, win2, win3)

    def to(leaf_at, near_at):
        return {"leaf": leaf_at, "near": near_at}

    def send_to(src, dst, send_sem, recv_sem, leaf_at, near_at):
        return pltpu.make_async_remote_copy(
            src_ref=src, dst_ref=dst, send_sem=send_sem, recv_sem=recv_sem,
            device_id=to(leaf_at, near_at), device_id_type=MESH,
        )

    def near_at(step):
        return lax.rem(near + step, NEAR)

    def leaf_at(step):
        return lax.rem(leaf + step + PLANE * PLANES, PLANE * PLANES)

    def plane_peer(step):
        return plane * PLANE + lax.rem(place + step, PLANE)

    def depth_peer(step):
        return lax.rem(plane + step + PLANES, PLANES) * PLANE + place

    loads = {}
    for number, (name, src, dst) in enumerate((
        ("pos", pos_in, pos_ref), ("dir", dir_in, dir_ref), ("basis", basis_in, basis_ref),
        ("btrans", btrans_in, btrans_ref), ("lskel", lskel_in, lskel_ref), ("ltrans", ltrans_in, ltrans_ref),
        ("bskel", bskel_in, bskel_ref), ("noise", noise_in, noise_ref), ("res", res_in, res_ref),
        ("sol", sol_in, sol_ref),
    )):
        loads[name] = pltpu.make_async_copy(src, dst, in_sem.at[number])
        loads[name].start()

    barrier = pltpu.get_barrier_semaphore()

    def greet(leaf_to, near_to):
        pl.semaphore_signal(barrier, inc=1, device_id=to(leaf_to, near_to), device_id_type=MESH)

    for way in (1, -1):
        for step in range(NEAR):
            greet(leaf_at(way), near_at(step))

    @pl.loop(1, PLANE)
    def _(step):
        greet(plane_peer(step), near)

    @pl.loop(1, PLANES * NEAR)
    def _(step):
        greet(depth_peer(step // NEAR), near_at(lax.rem(step, NEAR)))

    count = count_ref[0]
    loads["pos"].wait()
    loads["dir"].wait()
    occupied = lax.broadcasted_iota(jnp.int32, (CAP, 128), 0) < count
    direction = jnp.where(occupied, dir_ref[...], 0.0)
    for component in range(3):
        win0[pl.ds(96 + component, CAP, stride=4), :] = pos_ref[component] * SCALE
    win0[pl.ds(99, CAP, stride=4), :] = direction

    pl.semaphore_wait(barrier, 8 + PLANE - 1 + PLANES * NEAR - 1)

    own = win0.at[pl.ds(96, 96), :]
    window_copies = {}
    number = 0
    for way, group in ((1, 0), (-1, 2), (0, 1)):
        for step in range(NEAR):
            if way == 0 and step == 0:
                continue
            chunk = (NEAR - step) % NEAR
            window_copies[way, step] = send_to(
                own, wins[chunk].at[pl.ds(96 * group, 96), :], win_s.at[number], win_r.at[number],
                leaf_at(way), near_at(step),
            )
            number += 1
    for way in (1, -1):
        window_copies[way, 0].start()

    loads["btrans"].wait()
    def packed(matrix):
        return jnp.concatenate([matrix[0:32], matrix[32:64]], axis=1)

    def ancestor(level):
        if level == 0:
            return btrans_ref[0, 0]
        both = pbuf[level - 1]
        return jnp.concatenate([both[:, 0:64], both[:, 64:128]], axis=0)

    pair_copies = []
    for level, first in ((2, 0), (3, 1), (4, 4)):
        span = 2 ** (level - 1)
        for step in range(1, span):
            pair_copies.append((span, send_to(
                psend.at[level - 1], pbuf.at[level - 1], p_s.at[first + step - 1], p_r.at[level - 2],
                leaf_at(2 * step), near,
            )))
    relay = send_to(pbuf, pbuf, relay_s, relay_r, leaf_at(1), near)

    @pl.when(core == 0)
    def _():
        pbuf[0] = packed(btrans_ref[0, 1])
        for level in (2, 3, 4):
            @pl.when(lax.rem(across, 2 ** (level - 1)) == 0)
            def _(level=level):
                psend[level - 1] = packed(btrans_ref[0, level])
                pbuf[level - 1] = psend[level - 1]
                for span, copy in pair_copies:
                    if span == 2 ** (level - 1):
                        copy.start()

    loads["basis"].wait()
    lanes64 = lax.broadcasted_iota(jnp.int32, (64, 128), 1)

    def one_coeff(slot, columns):
        product = basis_ref[slot] * jnp.where(slot < count, dir_ref[pl.ds(slot, 1), :], 0.0)
        return jnp.where(lanes64 == slot, jnp.sum(product, axis=1, keepdims=True), columns)

    columns = lax.fori_loop(0, CAP, one_coeff, jnp.zeros((64, 128), F32), unroll=4)
    cbuf[near] = padded_square(columns).T[0:CAP, 0:64]
    c_copies = []
    for step in range(1, NEAR):
        copy = send_to(cbuf.at[near], cbuf.at[near], c_s.at[step - 1], c_r.at[step - 1], leaf, near_at(step))
        copy.start()
        c_copies.append(copy)
    for way in (0, 1, -1):
        for step in range(1, NEAR):
            window_copies[way, step].start()

    sub = lax.broadcasted_iota(jnp.int32, (8, 128), 0)
    centre = jnp.zeros((8, 128), F32)
    for component in range(3):
        middle = jnp.mean(pos_ref[component]) * SCALE
        centre = jnp.where((sub == component) | (sub == component + 4), middle, centre)

    def extended(tile):
        square = tile * tile
        norm = square[0:1] + square[1:2] + square[2:3]
        return norm

    def prepare_target(pair, carry):
        tile = win0[pl.ds(pl.multiple_of(96 + 8 * pair, 8), 8), :] - centre
        for half in range(2):
            base = tile if half == 0 else pltpu.roll(tile, 4, 0)
            norm = extended(base)
            rows = jnp.where(sub < 3, -2.0 * base, jnp.where(sub == 3, 1.0, jnp.where(sub == 4, norm, 0.0)))
            high, middle, low = pieces(rows)
            stacked = jnp.concatenate(
                [high, high, middle, middle, high, low, jnp.zeros((128 - SPLIT_ROWS, 128), F32)], axis=0
            )
            tsplit[2 * pair + half] = stacked.T[:, 0:SPLIT_ROWS].astype(BF16)
        return carry

    lax.fori_loop(0, CAP // 2, prepare_target, 0)

    def prepare_sources(window, split, weights, at, lanes):
        split[3 * CAP, :, lanes] = jnp.zeros((SPLIT_ROWS, 128), BF16)
        weights[3 * CAP, at] = jnp.zeros((8, 128), F32)

        def one(pair, carry):
            tile = window[pl.ds(pl.multiple_of(8 * pair, 8), 8), :] - centre
            for half in range(2):
                base = tile if half == 0 else pltpu.roll(tile, 4, 0)
                norm = extended(base)
                rows = jnp.where(sub < 3, base, jnp.where(sub == 3, norm, jnp.where(sub == 4, 1.0, 0.0)))
                high, middle, low = pieces(rows)
                stacked = jnp.concatenate([high, middle, high, middle, low, high], axis=0)
                split[2 * pair + half, :, lanes] = stacked.astype(BF16)
                weights[2 * pair + half, at] = jnp.broadcast_to(base[3:4], (8, 128))
            return carry

        lax.fori_loop(0, 3 * CAP // 2, one, 0, unroll=2)

    for name in ("lskel", "ltrans", "bskel", "noise", "res", "sol"):
        loads[name].wait()
    skeleton_rows = padded_square(
        jnp.concatenate([lskel_ref[0], lskel_ref[1], lskel_ref[2]], axis=0) * SCALE
    ).T
    for row in range(3 * CAP):
        ftarget[row] = jnp.broadcast_to(skeleton_rows[0:64, row:row + 1], (64, 64))
    for component in range(3):
        farwin[component, CAP:2 * CAP, :] = lskel_ref[component] * SCALE
    farwin[:, 3 * CAP:, :] = jnp.zeros((4, 8, 64), F32)

    for copy in c_copies:
        copy.wait_recv()
    coeffs = cbuf[0] + cbuf[1] + cbuf[2] + cbuf[3]
    farwin[3, CAP:2 * CAP, :] = coeffs
    l_copies = []
    for number, (way, group) in enumerate(((1, 0), (-1, 2))):
        copy = send_to(
            farwin.at[:, pl.ds(CAP, CAP), :], farwin.at[:, pl.ds(CAP * group, CAP), :],
            l_s.at[number], l_r.at[number], leaf_at(way), near,
        )
        copy.start()
        l_copies.append(copy)

    for level in (2, 3, 4):
        @pl.when((core == 0) & (lax.rem(across, 2 ** (level - 1)) != 0))
        def _(level=level):
            send_to(
                psend.at[level - 1], pbuf.at[level - 1], p_s.at[0], p_r.at[level - 2], leaf, near
            ).wait_recv()

    @pl.when(core == 0)
    def _():
        relay.start()

    total = jnp.zeros((64, 64), F32)
    for slot in range(CAP):
        total = total + ltrans_ref[slot] * farwin[3, CAP + slot:CAP + slot + 1, :]
    lifted = padded_square(jnp.broadcast_to(jnp.sum(total, axis=1, keepdims=True), (64, 128))).T[0:1, 0:64]

    @pl.when(core == 1)
    def _():
        relay.wait_recv()

    bufa[place] = jnp.zeros((16, 128), F32)
    bufa[place, 0:1, 0:64] = lifted
    for level in range(LEVELS - 1):
        lifted = row_times(lifted, ancestor(level), True)
        bufa[place, level + 1:level + 2, 0:64] = lifted
    for component, (row, lane) in enumerate(((0, 64), (8, 0), (8, 64))):
        bufa[place, row:row + LEVELS, lane:lane + 64] = bskel_ref[component, :, 0, :] * SCALE

    def a_copy(step):
        return send_to(bufa.at[place], bufa.at[place], a_s.at[step], a_r.at[step], plane_peer(step), near)

    @pl.loop(1, PLANE)
    def _(step):
        a_copy(step).start()

    def near_slots(low, high, split, weights, width, first, slots):
        chunks = [(k, j) for k in range(NEAR_NB) for j in range(width)]
        units = [chunks[i:i + 2] for i in range(0, len(chunks), 2)]

        def listed(slot, k):
            index = near_ref[k, slot]
            return jnp.where(index < 0, 3 * CAP, index)

        def buffer_of(u):
            return 0 if u == 0 else 1 + (u - 1) % 2

        def multiply(slot, u):
            parts = [split[listed(slot, k), :, 128 * j:128 * j + 128] for k, j in units[u]]
            sources = jnp.concatenate(parts, axis=1) if len(parts) > 1 else parts[0]
            products[buffer_of(u), :, 0:128 * len(parts)] = jnp.dot(
                tsplit[slot], sources, preferred_element_type=F32
            )

        def some_slots(step, carry):
            start = low + step * slots
            work = [(start + i, u) for i in range(slots) for u in range(len(units))]
            following = jnp.minimum(start + slots, CAP - 1)
            sums = []
            for at, (slot, u) in enumerate(work):
                if u == 0:
                    if first:
                        sums = [jnp.zeros((8, 128), F32)] * 16
                    else:
                        sums = [acc[slot, 8 * g:8 * g + 8, :] for g in range(16)]
                next_slot, next_u = work[at + 1] if at + 1 < len(work) else (following, 0)
                multiply(next_slot, next_u)
                weight = [weights[listed(slot, k), j] for k, j in units[u]]
                for g in range(16):
                    for i in range(len(weight)):
                        tile = decay(products[buffer_of(u), 8 * g:8 * g + 8, 128 * i:128 * i + 128])
                        sums[g] = sums[g] + tile * weight[i]
                if u + 1 == len(units):
                    if first:
                        for g in range(16):
                            acc[slot, 8 * g:8 * g + 8, :] = sums[g]
                    else:
                        whole = jnp.concatenate(sums, axis=0).T
                        near_rows[pl.ds(slot, 1), :] = jnp.sum(whole, axis=0, keepdims=True)
            return carry

        multiply(low, 0)
        lax.fori_loop(0, (high - low) // slots, some_slots, 0)

    for way in (1, -1):
        window_copies[way, 0].wait_recv()
    prepare_sources(win0, split0, wb0, 0, slice(0, 128))
    near_slots(0, CAP, split0, wb0, 1, True, 4)

    @pl.loop(1, PLANE)
    def _(step):
        a_copy(step).wait_recv()

    low_lanes = lax.broadcasted_iota(jnp.int32, (1, 128), 1) < 64
    sums = [bufa[i, 0:8, :] for i in range(PLANE)]
    offset = 0
    for level in range(LEVELS):
        span = 2 ** min(level, 4)
        if 0 < level < 5:
            sums = [sums[2 * i] + sums[2 * i + 1] for i in range(len(sums) // 2)]
        for box in range(PLANE // span):
            own = bufa[box * span]
            rows = (
                jnp.where(low_lanes, sums[box][level:level + 1], own[level:level + 1]),
                own[8 + level:9 + level],
            )
            for half in range(2):
                if level < 3:
                    big[1, half, offset + box:offset + box + 1, :] = rows[half]
                else:
                    at = 4 * half + (0, 2, 3)[level - 3] + box
                    small[plane, at:at + 1, :] = rows[half]
        offset += PLANE // span

    def b_copy(step):
        return send_to(small.at[plane], small.at[plane], b_s.at[step], b_r.at[step], depth_peer(step), near)

    @pl.loop(1, PLANES)
    def _(step):
        b_copy(step).start()

    g_copies = []
    for number, (way, slot) in enumerate(((1, 0), (-1, 2))):
        copy = send_to(big.at[1], big.at[slot], g_s.at[number], g_r.at[number], depth_peer(way), near)
        copy.start()
        g_copies.append(copy)

    for way in (1, -1, 0):
        for step in range(1, NEAR):
            window_copies[way, step].wait_recv()
    for j in range(3):
        prepare_sources(wins[j + 1], split3, wb3, j, slice(128 * j, 128 * j + 128))
    near_slots(0, 8, split3, wb3, 3, False, 2)

    for copy in l_copies:
        copy.wait_recv()

    def one_far(slot, carry):
        target = [ftarget[c * CAP + slot] for c in range(3)]
        running = jnp.zeros((64, 64), F32)
        for k in range(2):
            index = far_ref[k, slot]
            index = jnp.where(index < 0, 3 * CAP, index)
            squared = jnp.zeros((64, 64), F32)
            for c in range(3):
                spacing = target[c] - farwin[c, pl.ds(index, 1), :]
                squared = squared + spacing * spacing
            running = running + decay(squared) * farwin[3, pl.ds(index, 1), :]
        return jnp.where(lanes64 == slot, jnp.sum(running, axis=1, keepdims=True), carry)

    far_columns = lax.fori_loop(0, CAP, one_far, jnp.zeros((64, 128), F32), unroll=6)
    fbuf[near] = padded_square(far_columns).T[0:CAP, 0:64] * AMPLITUDE
    f_copies = []
    for step in range(1, NEAR):
        copy = send_to(fbuf.at[near], fbuf.at[near], f_s.at[step - 1], f_r.at[step - 1], leaf, near_at(step))
        copy.start()
        f_copies.append(copy)

    @pl.loop(1, PLANES)
    def _(step):
        b_copy(step).wait_recv()

    for copy in g_copies:
        copy.wait_recv()
    targets[...] = jnp.zeros((128, 128), F32)
    for level in range(LEVELS):
        first = place // 2 ** level * 2 ** level
        for half in range(2):
            if level < 5:
                row = bufa[first, 8 * half + level:8 * half + level + 1, :]
            else:
                row = small[plane // 2 * 2, 4 * half + 3:4 * half + 4, :]
            targets[2 * level + half:2 * level + half + 1, :] = row
    turned = targets[...].T
    offsets = (0, 16, 24)
    field_columns = jnp.zeros((64, 128), F32)
    for level in range(LEVELS):
        box = leaf // 2 ** level
        boxes = PLANE * PLANES // 2 ** level
        target = [
            jnp.broadcast_to(turned[lane:lane + 64, 2 * level + half:2 * level + half + 1], (64, 64))
            for half, lane in ((0, 64), (1, 0), (1, 64))
        ]
        running = jnp.zeros((64, 64), F32)
        for away in (jnp.where(lax.rem(box, 2) == 1, -3, 3), -2, 2):
            other = box + away
            exists = (other >= 0) & (other < boxes)
            other = jnp.clip(other, 0, boxes - 1)
            if level < 3:
                each = PLANE // 2 ** level
                other_plane = other // each - plane + 1
                at = offsets[level] + lax.rem(other, each)
                halves = [big[other_plane, half, pl.ds(at, 1), :] for half in range(2)]
            elif level < 5:
                each = PLANE // 2 ** level
                at = (0, 2)[level - 3] + lax.rem(other, each)
                halves = [small[other // each, pl.ds(4 * half + at, 1), :] for half in range(2)]
            else:
                halves = [small[2 * other, 4 * half + 3:4 * half + 4, :] for half in range(2)]
                halves[0] = halves[0] + jnp.where(low_lanes, small[2 * other + 1, 3:4, :], 0.0)
            rows = [half[:, lane:lane + 64] for half in halves for lane in (0, 64)]
            squared = jnp.zeros((64, 64), F32)
            for c in range(3):
                spacing = target[c] - rows[c + 1]
                squared = squared + spacing * spacing
            running = running + decay(squared) * jnp.where(exists, rows[0], 0.0)
        field_columns = jnp.where(lanes64 == level, jnp.sum(running, axis=1, keepdims=True), field_columns)
    fields = padded_square(field_columns).T[0:8, 0:64] * AMPLITUDE
    downward = fields[LEVELS - 1:LEVELS]
    for level in range(LEVELS - 2, -1, -1):
        downward = fields[level:level + 1] + row_times(downward, ancestor(level), False)
    down_column = jnp.broadcast_to(
        jnp.concatenate([downward, jnp.zeros((1, 64), F32)], axis=1), (128, 128)
    ).T[0:64, 0:64]
    for slot in range(CAP):
        far_rows[slot:slot + 1, :] = jnp.sum(ltrans_ref[slot] * down_column, axis=0, keepdims=True)

    near_slots(8, 16, split3, wb3, 3, False, 2)

    for copy in f_copies:
        copy.wait_recv()
    expansion = far_rows[...] + (fbuf[0] + fbuf[1] + fbuf[2] + fbuf[3])
    expansion_columns = padded_square(expansion).T
    for slot in range(CAP):
        far_vals[slot:slot + 1, :] = jnp.sum(
            basis_ref[slot] * expansion_columns[0:64, slot:slot + 1], axis=0, keepdims=True
        )

    near_slots(16, CAP, split3, wb3, 3, False, 2)

    residual = jnp.where(occupied, res_ref[...], 0.0)
    image = jnp.where(
        occupied, noise_ref[...] * direction + AMPLITUDE * near_rows[...] + far_vals[...], 0.0
    )
    kept_sol_ref[...] = jnp.where(occupied, sol_ref[...], 0.0)
    kept_res_ref[...] = residual
    tile = jnp.zeros((8, 128), F32)
    for number, product in enumerate(
        (residual * residual, direction * image, residual * image, image * image)
    ):
        tile = jnp.where(sub == number, jnp.sum(product, axis=0, keepdims=True), tile)

    lane_group = lax.broadcasted_iota(jnp.int32, (8, 128), 1) // 32
    tile = tile + pltpu.roll(tile, 64, 1)
    tile = tile + pltpu.roll(tile, 32, 1)
    row = jnp.sum(jnp.where(sub == lane_group, tile, 0.0), axis=0, keepdims=True)

    mine = plane * NEAR + near
    hop1[mine] = row
    hop_copies = []
    for depth in range(PLANES):
        for step in range(NEAR):
            if depth or step:
                at = depth * NEAR + step
                copy = send_to(
                    hop1.at[mine], hop1.at[mine], h1_s.at[at], h1_r.at[at], depth_peer(depth), near_at(step)
                )
                copy.start()
                hop_copies.append(copy)
    for copy in hop_copies:
        copy.wait_recv()
    hop2[place] = jnp.sum(hop1[...], axis=0)
    last_copies = []
    for step in range(1, PLANE):
        copy = send_to(
            hop2.at[place], hop2.at[place], h2_s.at[step], h2_r.at[step], plane_peer(step), near
        )
        copy.start()
        last_copies.append(copy)
    for copy in last_copies:
        copy.wait_recv()
    row = jnp.sum(hop2[...], axis=0)
    totals = jnp.sum(jnp.where(sub == lane_group, row, 0.0), axis=1, keepdims=True)
    norm_old, curvature, mixed, image_norm = (totals[i:i + 1] for i in range(4))
    step_length = norm_old / curvature
    norm_new = norm_old - 2.0 * step_length * mixed + step_length * step_length * image_norm
    step_ref[...] = jnp.broadcast_to(step_length, (CAP, 128))
    res_step_ref[...] = step_length * image
    ratio_ref[...] = jnp.broadcast_to(norm_new / norm_old, (CAP, 128))
    kept_dir_ref[...] = direction

    for copy in window_copies.values():
        copy.wait_send()

    @pl.when(core == 0)
    def _():
        relay.wait_send()
        for level in (2, 3, 4):
            @pl.when(lax.rem(across, 2 ** (level - 1)) == 0)
            def _(level=level):
                for span, copy in pair_copies:
                    if span == 2 ** (level - 1):
                        copy.wait_send()

    for copy in c_copies + l_copies + g_copies + f_copies + hop_copies + last_copies:
        copy.wait_send()

    @pl.loop(1, PLANE)
    def _(step):
        a_copy(step).wait_send()

    @pl.loop(1, PLANES)
    def _(step):
        b_copy(step).wait_send()


def per_device(
    positions, noise_variance, solution, residual, direction, leaf_basis, leaf_skeleton,
    leaf_transfer, box_transfer, box_skeleton, leaf_count, near_list, far_list,
):
    vmem = pl.BlockSpec(memory_space=pltpu.VMEM)
    smem = pl.BlockSpec(memory_space=pltpu.SMEM)
    hbm = pl.BlockSpec(memory_space=pltpu.HBM)
    dma = pltpu.SemaphoreType.DMA
    slots = 3 * CAP + 1
    arrays = (
        positions, noise_variance, solution, residual, direction, leaf_basis, leaf_skeleton,
        leaf_transfer, box_transfer, box_skeleton.transpose(0, 2, 1, 3),
    )
    kept_solution, kept_residual, residual_step, kept_direction, step, ratio = pl.pallas_call(
        kernel,
        out_shape=(jax.ShapeDtypeStruct((CAP, 128), F32),) * 6,
        in_specs=[smem] * 3 + [hbm] * len(arrays),
        out_specs=(vmem,) * 6,
        scratch_shapes=[
            *[pltpu.VMEM(array.shape, F32) for array in arrays],
            dma((len(arrays),)),
            *[pltpu.VMEM((12 * CAP, 128), F32)] * 4,
            pltpu.VMEM((slots, SPLIT_ROWS, 128), BF16),
            pltpu.VMEM((slots, SPLIT_ROWS, 384), BF16),
            pltpu.VMEM((slots, 1, 8, 128), F32),
            pltpu.VMEM((slots, 3, 8, 128), F32),
            pltpu.VMEM((CAP, 128, SPLIT_ROWS), BF16),
            pltpu.VMEM((3, 128, 256), F32),
            pltpu.VMEM((CAP, 128, 128), F32),
            pltpu.VMEM((CAP, 128), F32),
            pltpu.VMEM((NEAR, CAP, 64), F32),
            pltpu.VMEM((NEAR, CAP, 64), F32),
            pltpu.VMEM((4, 3 * CAP + 8, 64), F32),
            pltpu.VMEM((3 * CAP, 64, 64), F32),
            pltpu.VMEM((4, 32, 128), F32),
            pltpu.VMEM((4, 32, 128), F32),
            pltpu.VMEM((PLANE, 16, 128), F32),
            pltpu.VMEM((3, 2, 32, 128), F32),
            pltpu.VMEM((PLANES, 8, 128), F32),
            pltpu.VMEM((CAP, 64), F32),
            pltpu.VMEM((CAP, 64), F32),
            pltpu.VMEM((CAP, 128), F32),
            pltpu.VMEM((128, 128), F32),
            pltpu.VMEM((NEAR * PLANES, 1, 128), F32),
            pltpu.VMEM((PLANE, 1, 128), F32),
            dma((11,)), dma((11,)), dma((3,)), dma((3,)), dma((2,)), dma((2,)),
            dma((11,)), dma((3,)), dma, dma, dma((PLANE,)), dma((PLANE,)),
            dma((PLANES,)), dma((PLANES,)), dma((2,)), dma((2,)),
            dma((3,)), dma((3,)), dma((NEAR * PLANES,)), dma((NEAR * PLANES,)),
            dma((PLANE,)), dma((PLANE,)),
        ],
        compiler_params=pltpu.CompilerParams(
            collective_id=0, has_side_effects=True, vmem_limit_bytes=64 * 2**20
        ),
        name="iteration",
    )(leaf_count, near_list.T, far_list.T, *arrays)
    new_residual = kept_residual - residual_step
    return kept_solution + step * kept_direction, new_residual, new_residual + ratio * kept_direction


def solution(mesh):
    return jax.shard_map(
        per_device,
        mesh=mesh,
        in_specs=(
            P(None, "leaf", "near"),
            P("leaf", "near"),
            P("leaf", "near"),
            P("leaf", "near"),
            P("leaf", "near"),
            P("leaf", None, "near"),
            P(None, "leaf", None),
            P("leaf", None, None),
            P("leaf", None, None, None),
            P(None, "leaf", None, None),
            P("leaf"),
            P("leaf", None),
            P("leaf", "near"),
        ),
        out_specs=(P("leaf", "near"), P("leaf", "near"), P("leaf", "near")),
        check_vma=False,
    )
```

```python
import functools

import jax
import jax.numpy as jnp
from jax import lax
from jax.experimental import pallas as pl
from jax.experimental.pallas import tpu as pltpu
from jax.sharding import PartitionSpec as P

AMPLITUDE = 0.02
SCALE = 2.0 * 1.4426950408889634
HIGHEST = lax.Precision.HIGHEST
MESH = pl.DeviceIdType.MESH
F32 = jnp.float32
BF16 = jnp.bfloat16
CAP = 24
NEAR = 4
PLANE = 16
PLANES = 8
NEAR_NB = 9
LEVELS = 6
SPLIT_ROWS = 48
TINY = 1e-12


def pieces(tile):
    high = tile.astype(BF16).astype(F32)
    rest = tile - high
    middle = rest.astype(BF16).astype(F32)
    return high, middle, rest - middle


def decay(squared):
    clamped = jnp.maximum(squared, TINY)
    return jnp.exp2(-(clamped * lax.rsqrt(clamped)))


def row_times(row, matrix, transposed):
    dims = (((1,), (1 if transposed else 0,)), ((), ()))
    wide = jnp.broadcast_to(row, (8, row.shape[1]))
    return lax.dot_general(
        wide, matrix, dims, precision=HIGHEST, preferred_element_type=F32
    )[0:1]


def padded_square(block):
    rows, lanes = block.shape
    if lanes < 128:
        block = jnp.concatenate([block, jnp.zeros((rows, 128 - lanes), F32)], axis=1)
    if rows < 128:
        block = jnp.concatenate([block, jnp.zeros((128 - rows, 128), F32)], axis=0)
    return block


def kernel(
    count_ref, near_ref, far_ref,
    pos_in, noise_in, sol_in, res_in, dir_in, basis_in, lskel_in, ltrans_in, btrans_in, bskel_in,
    kept_sol_ref, kept_res_ref, res_step_ref, kept_dir_ref, step_ref, ratio_ref,
    pos_ref, noise_ref, sol_ref, res_ref, dir_ref, basis_ref, lskel_ref, ltrans_ref, btrans_ref, bskel_ref, in_sem,
    win0, win1, win2, win3, split0, split3, wb0, wb3, tsplit, products, acc, near_rows,
    cbuf, fbuf, farwin, ftarget, psend, pbuf, bufa, big, small, far_rows, ebuf, far_vals, targets,
    hop1, hop2,
    win_s, win_r, c_s, c_r, l_s, l_r, p_s, p_r, relay_s, relay_r, a_s, a_r, b_s, b_r, g_s, g_r,
    f_s, f_r, h1_s, h1_r, h2_s, h2_r,
):
    leaf = lax.axis_index("leaf")
    near = lax.axis_index("near")
    plane = leaf // PLANE
    place = lax.rem(leaf, PLANE)
    across = place // 2
    core = lax.rem(place, 2)
    wins = (win0, win1, win2, win3)

    def to(leaf_at, near_at):
        return {"leaf": leaf_at, "near": near_at}

    def send_to(src, dst, send_sem, recv_sem, leaf_at, near_at):
        return pltpu.make_async_remote_copy(
            src_ref=src, dst_ref=dst, send_sem=send_sem, recv_sem=recv_sem,
            device_id=to(leaf_at, near_at), device_id_type=MESH,
        )

    def near_at(step):
        return lax.rem(near + step, NEAR)

    def leaf_at(step):
        return lax.rem(leaf + step + PLANE * PLANES, PLANE * PLANES)

    def plane_peer(step):
        return plane * PLANE + lax.rem(place + step, PLANE)

    def depth_peer(step):
        return lax.rem(plane + step + PLANES, PLANES) * PLANE + place

    barrier = pltpu.get_barrier_semaphore()

    def greet(leaf_to, near_to):
        pl.semaphore_signal(barrier, inc=1, device_id=to(leaf_to, near_to), device_id_type=MESH)

    for way in (1, -1):
        for step in range(NEAR):
            greet(leaf_at(way), near_at(step))

    @pl.loop(1, PLANE)
    def _(step):
        greet(plane_peer(step), near)

    @pl.loop(1, PLANES * NEAR)
    def _(step):
        greet(depth_peer(step // NEAR), near_at(lax.rem(step, NEAR)))

    loads = {}
    for number, (name, src, dst) in enumerate((
        ("pos", pos_in, pos_ref), ("dir", dir_in, dir_ref), ("basis", basis_in, basis_ref),
        ("btrans", btrans_in, btrans_ref), ("lskel", lskel_in, lskel_ref), ("ltrans", ltrans_in, ltrans_ref),
        ("bskel", bskel_in, bskel_ref), ("noise", noise_in, noise_ref), ("res", res_in, res_ref),
        ("sol", sol_in, sol_ref),
    )):
        loads[name] = pltpu.make_async_copy(src, dst, in_sem.at[number])
        loads[name].start()

    count = count_ref[0]
    loads["pos"].wait()
    loads["dir"].wait()
    occupied = lax.broadcasted_iota(jnp.int32, (CAP, 128), 0) < count
    direction = jnp.where(occupied, dir_ref[...], 0.0)
    for component in range(3):
        win0[pl.ds(96 + component, CAP, stride=4), :] = pos_ref[component] * SCALE
    win0[pl.ds(99, CAP, stride=4), :] = direction

    pl.semaphore_wait(barrier, 8 + PLANE - 1 + PLANES * NEAR - 1)

    own = win0.at[pl.ds(96, 96), :]
    window_copies = {}
    number = 0
    for way, group in ((1, 0), (-1, 2), (0, 1)):
        for step in range(NEAR):
            if way == 0 and step == 0:
                continue
            chunk = (NEAR - step) % NEAR
            window_copies[way, step] = send_to(
                own, wins[chunk].at[pl.ds(96 * group, 96), :], win_s.at[number], win_r.at[number],
                leaf_at(way), near_at(step),
            )
            number += 1
    for way in (1, -1):
        window_copies[way, 0].start()

    loads["btrans"].wait()
    def packed(matrix):
        return jnp.concatenate([matrix[0:32], matrix[32:64]], axis=1)

    def ancestor(level):
        if level == 0:
            return btrans_ref[0, 0]
        both = pbuf[level - 1]
        return jnp.concatenate([both[:, 0:64], both[:, 64:128]], axis=0)

    pair_copies = []
    for level, first in ((2, 0), (3, 1), (4, 4)):
        span = 2 ** (level - 1)
        for step in range(1, span):
            pair_copies.append((span, send_to(
                psend.at[level - 1], pbuf.at[level - 1], p_s.at[first + step - 1], p_r.at[level - 2],
                leaf_at(2 * step), near,
            )))
    relay = send_to(pbuf, pbuf, relay_s, relay_r, leaf_at(1), near)

    @pl.when(core == 0)
    def _():
        pbuf[0] = packed(btrans_ref[0, 1])
        for level in (2, 3, 4):
            @pl.when(lax.rem(across, 2 ** (level - 1)) == 0)
            def _(level=level):
                psend[level - 1] = packed(btrans_ref[0, level])
                pbuf[level - 1] = psend[level - 1]
                for span, copy in pair_copies:
                    if span == 2 ** (level - 1):
                        copy.start()

    loads["basis"].wait()
    lanes64 = lax.broadcasted_iota(jnp.int32, (64, 128), 1)

    def one_coeff(slot, columns):
        product = basis_ref[slot] * jnp.where(slot < count, dir_ref[pl.ds(slot, 1), :], 0.0)
        return jnp.where(lanes64 == slot, jnp.sum(product, axis=1, keepdims=True), columns)

    columns = lax.fori_loop(0, CAP, one_coeff, jnp.zeros((64, 128), F32), unroll=4)
    cbuf[near] = padded_square(columns).T[0:CAP, 0:64]
    c_copies = []
    for step in range(1, NEAR):
        copy = send_to(cbuf.at[near], cbuf.at[near], c_s.at[step - 1], c_r.at[step - 1], leaf, near_at(step))
        copy.start()
        c_copies.append(copy)
    for way in (0, 1, -1):
        for step in range(1, NEAR):
            window_copies[way, step].start()

    sub = lax.broadcasted_iota(jnp.int32, (8, 128), 0)
    centre = jnp.zeros((8, 128), F32)
    for component in range(3):
        middle = jnp.mean(pos_ref[component]) * SCALE
        centre = jnp.where((sub == component) | (sub == component + 4), middle, centre)

    def extended(tile):
        square = tile * tile
        norm = square[0:1] + square[1:2] + square[2:3]
        return norm

    def prepare_target(pair, carry):
        tile = win0[pl.ds(pl.multiple_of(96 + 8 * pair, 8), 8), :] - centre
        for half in range(2):
            base = tile if half == 0 else pltpu.roll(tile, 4, 0)
            norm = extended(base)
            rows = jnp.where(sub < 3, -2.0 * base, jnp.where(sub == 3, 1.0, jnp.where(sub == 4, norm, 0.0)))
            high, middle, low = pieces(rows)
            stacked = jnp.concatenate(
                [high, high, middle, middle, high, low, jnp.zeros((128 - SPLIT_ROWS, 128), F32)], axis=0
            )
            tsplit[2 * pair + half] = stacked.T[:, 0:SPLIT_ROWS].astype(BF16)
        return carry

    lax.fori_loop(0, CAP // 2, prepare_target, 0)

    def prepare_sources(window, split, weights, at, lanes):
        split[3 * CAP, :, lanes] = jnp.zeros((SPLIT_ROWS, 128), BF16)
        weights[3 * CAP, at] = jnp.zeros((8, 128), F32)

        def one(pair, carry):
            tile = window[pl.ds(pl.multiple_of(8 * pair, 8), 8), :] - centre
            for half in range(2):
                base = tile if half == 0 else pltpu.roll(tile, 4, 0)
                norm = extended(base)
                rows = jnp.where(sub < 3, base, jnp.where(sub == 3, norm, jnp.where(sub == 4, 1.0, 0.0)))
                high, middle, low = pieces(rows)
                stacked = jnp.concatenate([high, middle, high, middle, low, high], axis=0)
                split[2 * pair + half, :, lanes] = stacked.astype(BF16)
                weights[2 * pair + half, at] = jnp.broadcast_to(base[3:4], (8, 128))
            return carry

        lax.fori_loop(0, 3 * CAP // 2, one, 0, unroll=2)

    for name in ("lskel", "ltrans", "bskel", "noise", "res", "sol"):
        loads[name].wait()
    skeleton_rows = padded_square(
        jnp.concatenate([lskel_ref[0], lskel_ref[1], lskel_ref[2]], axis=0) * SCALE
    ).T
    for row in range(3 * CAP):
        ftarget[row] = jnp.broadcast_to(skeleton_rows[0:64, row:row + 1], (64, 64))
    for component in range(3):
        farwin[component, CAP:2 * CAP, :] = lskel_ref[component] * SCALE
    farwin[:, 3 * CAP:, :] = jnp.zeros((4, 8, 64), F32)

    def near_slots(low, high, split, weights, width, first, slots, inline=False):
        chunks = [(k, j) for k in range(NEAR_NB) for j in range(width)]
        units = [chunks[i:i + 2] for i in range(0, len(chunks), 2)]

        def listed(slot, k):
            index = near_ref[k, slot]
            return jnp.where(index < 0, 3 * CAP, index)

        def buffer_of(u):
            return 0 if u == 0 else 1 + (u - 1) % 2

        def multiply(slot, u):
            parts = [split[listed(slot, k), :, 128 * j:128 * j + 128] for k, j in units[u]]
            sources = jnp.concatenate(parts, axis=1) if len(parts) > 1 else parts[0]
            products[buffer_of(u), :, 0:128 * len(parts)] = jnp.dot(
                tsplit[slot], sources, preferred_element_type=F32
            )

        def some_slots(step, carry):
            start = low + step * slots
            work = [(start + i, u) for i in range(slots) for u in range(len(units))]
            following = jnp.minimum(start + slots, CAP - 1)
            sums = []
            for at, (slot, u) in enumerate(work):
                if u == 0:
                    if first:
                        sums = [jnp.zeros((8, 128), F32)] * 16
                    else:
                        sums = [acc[slot, 8 * g:8 * g + 8, :] for g in range(16)]
                next_slot, next_u = work[at + 1] if at + 1 < len(work) else (following, 0)
                multiply(next_slot, next_u)
                weight = [weights[listed(slot, k), j] for k, j in units[u]]
                for g in range(16):
                    for i in range(len(weight)):
                        tile = decay(products[buffer_of(u), 8 * g:8 * g + 8, 128 * i:128 * i + 128])
                        sums[g] = sums[g] + tile * weight[i]
                if u + 1 == len(units):
                    if first:
                        for g in range(16):
                            acc[slot, 8 * g:8 * g + 8, :] = sums[g]
                    else:
                        whole = jnp.concatenate(sums, axis=0).T
                        near_rows[pl.ds(slot, 1), :] = jnp.sum(whole, axis=0, keepdims=True)
            return carry

        multiply(low, 0)
        if inline:
            some_slots(0, 0)
        else:
            lax.fori_loop(0, (high - low) // slots, some_slots, 0)

    for way in (1, -1):
        window_copies[way, 0].wait_recv()
    prepare_sources(win0, split0, wb0, 0, slice(0, 128))
    near_slots(0, 20, split0, wb0, 1, True, 4)

    for level in (2, 3, 4):
        @pl.when((core == 0) & (lax.rem(across, 2 ** (level - 1)) != 0))
        def _(level=level):
            send_to(
                psend.at[level - 1], pbuf.at[level - 1], p_s.at[0], p_r.at[level - 2], leaf, near
            ).wait_recv()

    @pl.when(core == 0)
    def _():
        relay.start()

    for copy in c_copies:
        copy.wait_recv()
    coeffs = cbuf[0] + cbuf[1] + cbuf[2] + cbuf[3]
    farwin[3, CAP:2 * CAP, :] = coeffs
    l_copies = []
    for number, (way, group) in enumerate(((1, 0), (-1, 2))):
        copy = send_to(
            farwin.at[:, pl.ds(CAP, CAP), :], farwin.at[:, pl.ds(CAP * group, CAP), :],
            l_s.at[number], l_r.at[number], leaf_at(way), near,
        )
        copy.start()
        l_copies.append(copy)

    total = jnp.zeros((64, 64), F32)
    for slot in range(CAP):
        total = total + ltrans_ref[slot] * farwin[3, CAP + slot:CAP + slot + 1, :]
    lifted = padded_square(jnp.broadcast_to(jnp.sum(total, axis=1, keepdims=True), (64, 128))).T[0:1, 0:64]

    @pl.when(core == 1)
    def _():
        relay.wait_recv()

    near_slots(20, CAP, split0, wb0, 1, True, 4, inline=True)
    bufa[place] = jnp.zeros((16, 128), F32)
    bufa[place, 0:1, 0:64] = lifted
    for level in range(LEVELS - 1):
        lifted = row_times(lifted, ancestor(level), True)
        bufa[place, level + 1:level + 2, 0:64] = lifted
    for component, (row, lane) in enumerate(((0, 64), (8, 0), (8, 64))):
        bufa[place, row:row + LEVELS, lane:lane + 64] = bskel_ref[component, :, 0, :] * SCALE

    def a_copy(step):
        return send_to(bufa.at[place], bufa.at[place], a_s.at[step], a_r.at[step], plane_peer(step), near)

    @pl.loop(1, PLANE)
    def _(step):
        a_copy(step).start()

    for way in (1, -1, 0):
        for step in range(1, NEAR):
            window_copies[way, step].wait_recv()
    for j in range(3):
        prepare_sources(wins[j + 1], split3, wb3, j, slice(128 * j, 128 * j + 128))
    near_slots(0, 10, split3, wb3, 3, False, 2)

    @pl.loop(1, PLANE)
    def _(step):
        a_copy(step).wait_recv()

    low_lanes = lax.broadcasted_iota(jnp.int32, (1, 128), 1) < 64
    sums = [bufa[i, 0:8, :] for i in range(PLANE)]
    offset = 0
    for level in range(LEVELS):
        span = 2 ** min(level, 4)
        if 0 < level < 5:
            sums = [sums[2 * i] + sums[2 * i + 1] for i in range(len(sums) // 2)]
        for box in range(PLANE // span):
            own = bufa[box * span]
            rows = (
                jnp.where(low_lanes, sums[box][level:level + 1], own[level:level + 1]),
                own[8 + level:9 + level],
            )
            for half in range(2):
                if level < 3:
                    big[1, half, offset + box:offset + box + 1, :] = rows[half]
                else:
                    at = 4 * half + (0, 2, 3)[level - 3] + box
                    small[plane, at:at + 1, :] = rows[half]
        offset += PLANE // span

    def b_copy(step):
        return send_to(small.at[plane], small.at[plane], b_s.at[step], b_r.at[step], depth_peer(step), near)

    @pl.loop(1, PLANES)
    def _(step):
        b_copy(step).start()

    g_copies = []
    for number, (way, slot) in enumerate(((1, 0), (-1, 2))):
        copy = send_to(big.at[1], big.at[slot], g_s.at[number], g_r.at[number], depth_peer(way), near)
        copy.start()
        g_copies.append(copy)

    near_slots(10, 14, split3, wb3, 3, False, 2)

    for copy in l_copies:
        copy.wait_recv()

    def one_far(slot, carry):
        target = [ftarget[c * CAP + slot] for c in range(3)]
        running = jnp.zeros((64, 64), F32)
        for k in range(2):
            index = far_ref[k, slot]
            index = jnp.where(index < 0, 3 * CAP, index)
            squared = jnp.zeros((64, 64), F32)
            for c in range(3):
                spacing = target[c] - farwin[c, pl.ds(index, 1), :]
                squared = squared + spacing * spacing
            running = running + decay(squared) * farwin[3, pl.ds(index, 1), :]
        return jnp.where(lanes64 == slot, jnp.sum(running, axis=1, keepdims=True), carry)

    near_slots(14, 18, split3, wb3, 3, False, 4, inline=True)
    far_columns = jnp.zeros((64, 128), F32)
    for slot in range(CAP):
        far_columns = one_far(slot, far_columns)
    fbuf[near] = padded_square(far_columns).T[0:CAP, 0:64] * AMPLITUDE
    f_copies = []
    for step in range(1, NEAR):
        copy = send_to(fbuf.at[near], fbuf.at[near], f_s.at[step - 1], f_r.at[step - 1], leaf, near_at(step))
        copy.start()
        f_copies.append(copy)

    @pl.loop(1, PLANES)
    def _(step):
        b_copy(step).wait_recv()

    for copy in g_copies:
        copy.wait_recv()
    near_slots(18, 22, split3, wb3, 3, False, 4, inline=True)
    targets[...] = jnp.zeros((128, 128), F32)
    for level in range(LEVELS):
        first = place // 2 ** level * 2 ** level
        for half in range(2):
            if level < 5:
                row = bufa[first, 8 * half + level:8 * half + level + 1, :]
            else:
                row = small[plane // 2 * 2, 4 * half + 3:4 * half + 4, :]
            targets[2 * level + half:2 * level + half + 1, :] = row
    turned = targets[...].T
    offsets = (0, 16, 24)
    field_columns = jnp.zeros((64, 128), F32)
    for level in range(LEVELS):
        box = leaf // 2 ** level
        boxes = PLANE * PLANES // 2 ** level
        target = [
            jnp.broadcast_to(turned[lane:lane + 64, 2 * level + half:2 * level + half + 1], (64, 64))
            for half, lane in ((0, 64), (1, 0), (1, 64))
        ]
        running = jnp.zeros((64, 64), F32)
        for away in (jnp.where(lax.rem(box, 2) == 1, -3, 3), -2, 2):
            other = box + away
            exists = (other >= 0) & (other < boxes)
            other = jnp.clip(other, 0, boxes - 1)
            if level < 3:
                each = PLANE // 2 ** level
                other_plane = other // each - plane + 1
                at = offsets[level] + lax.rem(other, each)
                halves = [big[other_plane, half, pl.ds(at, 1), :] for half in range(2)]
            elif level < 5:
                each = PLANE // 2 ** level
                at = (0, 2)[level - 3] + lax.rem(other, each)
                halves = [small[other // each, pl.ds(4 * half + at, 1), :] for half in range(2)]
            else:
                halves = [small[2 * other, 4 * half + 3:4 * half + 4, :] for half in range(2)]
                halves[0] = halves[0] + jnp.where(low_lanes, small[2 * other + 1, 3:4, :], 0.0)
            rows = [half[:, lane:lane + 64] for half in halves for lane in (0, 64)]
            squared = jnp.zeros((64, 64), F32)
            for c in range(3):
                spacing = target[c] - rows[c + 1]
                squared = squared + spacing * spacing
            running = running + decay(squared) * jnp.where(exists, rows[0], 0.0)
        field_columns = jnp.where(lanes64 == level, jnp.sum(running, axis=1, keepdims=True), field_columns)
    fields = padded_square(field_columns).T[0:8, 0:64] * AMPLITUDE
    downward = fields[LEVELS - 1:LEVELS]
    for level in range(LEVELS - 2, -1, -1):
        downward = fields[level:level + 1] + row_times(downward, ancestor(level), False)
    down_column = jnp.broadcast_to(
        jnp.concatenate([downward, jnp.zeros((1, 64), F32)], axis=1), (128, 128)
    ).T[0:64, 0:64]
    for slot in range(CAP):
        far_rows[slot:slot + 1, :] = jnp.sum(ltrans_ref[slot] * down_column, axis=0, keepdims=True)


    for copy in f_copies:
        copy.wait_recv()
    near_slots(22, CAP, split3, wb3, 3, False, 2, inline=True)
    expansion = far_rows[...] + (fbuf[0] + fbuf[1] + fbuf[2] + fbuf[3])
    expansion_columns = padded_square(expansion).T
    for slot in range(CAP):
        far_vals[slot:slot + 1, :] = jnp.sum(
            basis_ref[slot] * expansion_columns[0:64, slot:slot + 1], axis=0, keepdims=True
        )

    residual = jnp.where(occupied, res_ref[...], 0.0)
    image = jnp.where(
        occupied, noise_ref[...] * direction + AMPLITUDE * near_rows[...] + far_vals[...], 0.0
    )
    kept_sol_ref[...] = jnp.where(occupied, sol_ref[...], 0.0)
    kept_res_ref[...] = residual
    tile = jnp.zeros((8, 128), F32)
    for number, product in enumerate(
        (residual * residual, direction * image, residual * image, image * image)
    ):
        tile = jnp.where(sub == number, jnp.sum(product, axis=0, keepdims=True), tile)

    lane_group = lax.broadcasted_iota(jnp.int32, (8, 128), 1) // 32
    tile = tile + pltpu.roll(tile, 64, 1)
    tile = tile + pltpu.roll(tile, 32, 1)
    row = jnp.sum(jnp.where(sub == lane_group, tile, 0.0), axis=0, keepdims=True)

    mine = plane * NEAR + near
    hop1[mine] = row
    hop_copies = []
    for depth in range(PLANES):
        for step in range(NEAR):
            if depth or step:
                at = depth * NEAR + step
                copy = send_to(
                    hop1.at[mine], hop1.at[mine], h1_s.at[at], h1_r.at[at], depth_peer(depth), near_at(step)
                )
                copy.start()
                hop_copies.append(copy)
    for copy in hop_copies:
        copy.wait_recv()
    hop2[place] = jnp.sum(hop1[...], axis=0)
    last_copies = []
    for step in range(1, PLANE):
        copy = send_to(
            hop2.at[place], hop2.at[place], h2_s.at[step], h2_r.at[step], plane_peer(step), near
        )
        copy.start()
        last_copies.append(copy)
    for copy in last_copies:
        copy.wait_recv()
    row = jnp.sum(hop2[...], axis=0)
    totals = jnp.sum(jnp.where(sub == lane_group, row, 0.0), axis=1, keepdims=True)
    norm_old, curvature, mixed, image_norm = (totals[i:i + 1] for i in range(4))
    step_length = norm_old / curvature
    norm_new = norm_old - 2.0 * step_length * mixed + step_length * step_length * image_norm
    step_ref[...] = jnp.broadcast_to(step_length, (CAP, 128))
    res_step_ref[...] = step_length * image
    ratio_ref[...] = jnp.broadcast_to(norm_new / norm_old, (CAP, 128))
    kept_dir_ref[...] = direction

    for copy in window_copies.values():
        copy.wait_send()

    @pl.when(core == 0)
    def _():
        relay.wait_send()
        for level in (2, 3, 4):
            @pl.when(lax.rem(across, 2 ** (level - 1)) == 0)
            def _(level=level):
                for span, copy in pair_copies:
                    if span == 2 ** (level - 1):
                        copy.wait_send()

    for copy in c_copies + l_copies + g_copies + f_copies + hop_copies + last_copies:
        copy.wait_send()

    @pl.loop(1, PLANE)
    def _(step):
        a_copy(step).wait_send()

    @pl.loop(1, PLANES)
    def _(step):
        b_copy(step).wait_send()


def per_device(
    positions, noise_variance, solution, residual, direction, leaf_basis, leaf_skeleton,
    leaf_transfer, box_transfer, box_skeleton, leaf_count, near_list, far_list,
):
    vmem = pl.BlockSpec(memory_space=pltpu.VMEM)
    smem = pl.BlockSpec(memory_space=pltpu.SMEM)
    hbm = pl.BlockSpec(memory_space=pltpu.HBM)
    dma = pltpu.SemaphoreType.DMA
    slots = 3 * CAP + 1
    arrays = (
        positions, noise_variance, solution, residual, direction, leaf_basis, leaf_skeleton,
        leaf_transfer, box_transfer, box_skeleton.transpose(0, 2, 1, 3),
    )
    kept_solution, kept_residual, residual_step, kept_direction, step, ratio = pl.pallas_call(
        kernel,
        out_shape=(jax.ShapeDtypeStruct((CAP, 128), F32),) * 6,
        in_specs=[smem] * 3 + [hbm] * len(arrays),
        out_specs=(vmem,) * 6,
        scratch_shapes=[
            *[pltpu.VMEM(array.shape, F32) for array in arrays],
            dma((len(arrays),)),
            *[pltpu.VMEM((12 * CAP, 128), F32)] * 4,
            pltpu.VMEM((slots, SPLIT_ROWS, 128), BF16),
            pltpu.VMEM((slots, SPLIT_ROWS, 384), BF16),
            pltpu.VMEM((slots, 1, 8, 128), F32),
            pltpu.VMEM((slots, 3, 8, 128), F32),
            pltpu.VMEM((CAP, 128, SPLIT_ROWS), BF16),
            pltpu.VMEM((3, 128, 256), F32),
            pltpu.VMEM((CAP, 128, 128), F32),
            pltpu.VMEM((CAP, 128), F32),
            pltpu.VMEM((NEAR, CAP, 64), F32),
            pltpu.VMEM((NEAR, CAP, 64), F32),
            pltpu.VMEM((4, 3 * CAP + 8, 64), F32),
            pltpu.VMEM((3 * CAP, 64, 64), F32),
            pltpu.VMEM((4, 32, 128), F32),
            pltpu.VMEM((4, 32, 128), F32),
            pltpu.VMEM((PLANE, 16, 128), F32),
            pltpu.VMEM((3, 2, 32, 128), F32),
            pltpu.VMEM((PLANES, 8, 128), F32),
            pltpu.VMEM((CAP, 64), F32),
            pltpu.VMEM((CAP, 64), F32),
            pltpu.VMEM((CAP, 128), F32),
            pltpu.VMEM((128, 128), F32),
            pltpu.VMEM((NEAR * PLANES, 1, 128), F32),
            pltpu.VMEM((PLANE, 1, 128), F32),
            dma((11,)), dma((11,)), dma((3,)), dma((3,)), dma((2,)), dma((2,)),
            dma((11,)), dma((3,)), dma, dma, dma((PLANE,)), dma((PLANE,)),
            dma((PLANES,)), dma((PLANES,)), dma((2,)), dma((2,)),
            dma((3,)), dma((3,)), dma((NEAR * PLANES,)), dma((NEAR * PLANES,)),
            dma((PLANE,)), dma((PLANE,)),
        ],
        compiler_params=pltpu.CompilerParams(
            collective_id=0, has_side_effects=True, vmem_limit_bytes=64 * 2**20
        ),
        name="iteration",
    )(leaf_count, near_list.T, far_list.T, *arrays)
    new_residual = kept_residual - residual_step
    return kept_solution + step * kept_direction, new_residual, new_residual + ratio * kept_direction


def solution(mesh):
    return jax.shard_map(
        per_device,
        mesh=mesh,
        in_specs=(
            P(None, "leaf", "near"),
            P("leaf", "near"),
            P("leaf", "near"),
            P("leaf", "near"),
            P("leaf", "near"),
            P("leaf", None, "near"),
            P(None, "leaf", None),
            P("leaf", None, None),
            P("leaf", None, None, None),
            P(None, "leaf", None, None),
            P("leaf"),
            P("leaf", None),
            P("leaf", "near"),
        ),
        out_specs=(P("leaf", "near"), P("leaf", "near"), P("leaf", "near")),
        check_vma=False,
    )
```

```python
import functools

import jax
import jax.numpy as jnp
from jax import lax
from jax.experimental import pallas as pl
from jax.experimental.pallas import tpu as pltpu
from jax.sharding import PartitionSpec as P

AMPLITUDE = 0.02
SCALE = 2.0 * 1.4426950408889634
HIGHEST = lax.Precision.HIGHEST
MESH = pl.DeviceIdType.MESH
F32 = jnp.float32
BF16 = jnp.bfloat16
CAP = 24
NEAR = 4
PLANE = 16
PLANES = 8
NEAR_NB = 9
LEVELS = 6
SPLIT_ROWS = 32
TINY = 1e-12


def pieces(tile):
    high = tile.astype(BF16).astype(F32)
    rest = tile - high
    middle = rest.astype(BF16).astype(F32)
    return high, middle, rest - middle


def decay(squared):
    clamped = jnp.maximum(squared, TINY)
    return jnp.exp2(-(clamped * lax.rsqrt(clamped)))


def row_times(row, matrix, transposed):
    dims = (((1,), (1 if transposed else 0,)), ((), ()))
    wide = jnp.broadcast_to(row, (8, row.shape[1]))
    return lax.dot_general(
        wide, matrix, dims, precision=HIGHEST, preferred_element_type=F32
    )[0:1]


def padded_square(block):
    rows, lanes = block.shape
    if lanes < 128:
        block = jnp.concatenate([block, jnp.zeros((rows, 128 - lanes), F32)], axis=1)
    if rows < 128:
        block = jnp.concatenate([block, jnp.zeros((128 - rows, 128), F32)], axis=0)
    return block


def kernel(
    count_ref, near_ref, far_ref,
    pos_in, noise_in, sol_in, res_in, dir_in, basis_in, lskel_in, ltrans_in, btrans_in, bskel_in,
    result_ref,
    pos_ref, noise_ref, sol_ref, res_ref, dir_ref, basis_ref, lskel_ref, ltrans_ref, btrans_ref, bskel_ref, in_sem,
    win0, win1, win2, win3, split0, split3, wb0, wb3, tsplit, products, acc, near_rows,
    cbuf, fbuf, farwin, ftarget, psend, pbuf, bufa, big, small, far_rows, ebuf, far_vals, targets,
    hop1, hop2,
    win_s, win_r, c_s, c_r, l_s, l_r, p_s, p_r, relay_s, relay_r, a_s, a_r, b_s, b_r, g_s, g_r,
    f_s, f_r, h1_s, h1_r, h2_s, h2_r,
):
    leaf = lax.axis_index("leaf")
    near = lax.axis_index("near")
    plane = leaf // PLANE
    place = lax.rem(leaf, PLANE)
    across = place // 2
    core = lax.rem(place, 2)
    wins = (win0, win1, win2, win3)

    def to(leaf_at, near_at):
        return {"leaf": leaf_at, "near": near_at}

    def send_to(src, dst, send_sem, recv_sem, leaf_at, near_at):
        return pltpu.make_async_remote_copy(
            src_ref=src, dst_ref=dst, send_sem=send_sem, recv_sem=recv_sem,
            device_id=to(leaf_at, near_at), device_id_type=MESH,
        )

    def near_at(step):
        return lax.rem(near + step, NEAR)

    def leaf_at(step):
        return lax.rem(leaf + step + PLANE * PLANES, PLANE * PLANES)

    def plane_peer(step):
        return plane * PLANE + lax.rem(place + step, PLANE)

    def depth_peer(step):
        return lax.rem(plane + step + PLANES, PLANES) * PLANE + place

    barrier = pltpu.get_barrier_semaphore()

    def greet(leaf_to, near_to):
        pl.semaphore_signal(barrier, inc=1, device_id=to(leaf_to, near_to), device_id_type=MESH)

    for way in (1, -1):
        for step in range(NEAR):
            greet(leaf_at(way), near_at(step))

    @pl.loop(1, PLANE)
    def _(step):
        greet(plane_peer(step), near)

    @pl.loop(1, PLANES * NEAR)
    def _(step):
        greet(depth_peer(step // NEAR), near_at(lax.rem(step, NEAR)))

    loads = {}
    for number, (name, src, dst) in enumerate((
        ("pos", pos_in, pos_ref), ("dir", dir_in, dir_ref), ("basis", basis_in, basis_ref),
        ("btrans", btrans_in, btrans_ref), ("lskel", lskel_in, lskel_ref), ("ltrans", ltrans_in, ltrans_ref),
        ("bskel", bskel_in, bskel_ref), ("noise", noise_in, noise_ref), ("res", res_in, res_ref),
        ("sol", sol_in, sol_ref),
    )):
        loads[name] = pltpu.make_async_copy(src, dst, in_sem.at[number])
        loads[name].start()

    count = count_ref[0]
    loads["pos"].wait()
    loads["dir"].wait()
    occupied = lax.broadcasted_iota(jnp.int32, (CAP, 128), 0) < count
    direction = jnp.where(occupied, dir_ref[...], 0.0)
    for component in range(3):
        win0[pl.ds(96 + component, CAP, stride=4), :] = pos_ref[component] * SCALE
    win0[pl.ds(99, CAP, stride=4), :] = direction

    loads["basis"].wait()
    lanes64 = lax.broadcasted_iota(jnp.int32, (64, 128), 1)

    def one_coeff(slot, columns):
        product = basis_ref[slot] * jnp.where(slot < count, dir_ref[pl.ds(slot, 1), :], 0.0)
        return jnp.where(lanes64 == slot, jnp.sum(product, axis=1, keepdims=True), columns)

    columns = lax.fori_loop(0, CAP, one_coeff, jnp.zeros((64, 128), F32), unroll=4)
    cbuf[near] = padded_square(columns).T[0:CAP, 0:64]

    pl.semaphore_wait(barrier, 8 + PLANE - 1 + PLANES * NEAR - 1)

    c_copies = []
    for step in range(1, NEAR):
        copy = send_to(cbuf.at[near], cbuf.at[near], c_s.at[step - 1], c_r.at[step - 1], leaf, near_at(step))
        copy.start()
        c_copies.append(copy)

    own = win0.at[pl.ds(96, 96), :]
    window_copies = {}
    number = 0
    for way, group in ((1, 0), (-1, 2), (0, 1)):
        for step in range(NEAR):
            if way == 0 and step == 0:
                continue
            chunk = (NEAR - step) % NEAR
            window_copies[way, step] = send_to(
                own, wins[chunk].at[pl.ds(96 * group, 96), :], win_s.at[number], win_r.at[number],
                leaf_at(way), near_at(step),
            )
            number += 1
    for way in (1, -1):
        window_copies[way, 0].start()

    loads["btrans"].wait()
    def packed(matrix):
        return jnp.concatenate([matrix[0:32], matrix[32:64]], axis=1)

    def ancestor(level):
        if level == 0:
            return btrans_ref[0, 0]
        both = pbuf[level - 1]
        return jnp.concatenate([both[:, 0:64], both[:, 64:128]], axis=0)

    pair_copies = []
    for level, first in ((2, 0), (3, 1), (4, 4)):
        span = 2 ** (level - 1)
        for step in range(1, span):
            pair_copies.append((span, send_to(
                psend.at[level - 1], pbuf.at[level - 1], p_s.at[first + step - 1], p_r.at[level - 2],
                leaf_at(2 * step), near,
            )))
    relay = send_to(pbuf, pbuf, relay_s, relay_r, leaf_at(1), near)

    @pl.when(core == 0)
    def _():
        pbuf[0] = packed(btrans_ref[0, 1])
        for level in (2, 3, 4):
            @pl.when(lax.rem(across, 2 ** (level - 1)) == 0)
            def _(level=level):
                psend[level - 1] = packed(btrans_ref[0, level])
                pbuf[level - 1] = psend[level - 1]
                for span, copy in pair_copies:
                    if span == 2 ** (level - 1):
                        copy.start()

    for way in (0, 1, -1):
        for step in range(1, NEAR):
            window_copies[way, step].start()

    sub = lax.broadcasted_iota(jnp.int32, (8, 128), 0)
    centre = jnp.zeros((8, 128), F32)
    for component in range(3):
        middle = jnp.mean(pos_ref[component]) * SCALE
        centre = jnp.where((sub == component) | (sub == component + 4), middle, centre)

    def extended(tile):
        square = tile * tile
        norm = square[0:1] + square[1:2] + square[2:3]
        return norm

    def prepare_target(pair, carry):
        tile = win0[pl.ds(pl.multiple_of(96 + 8 * pair, 8), 8), :] - centre
        for half in range(2):
            base = tile if half == 0 else pltpu.roll(tile, 4, 0)
            norm = extended(base)
            rows = jnp.where(sub < 3, -2.0 * base, jnp.where(sub == 3, 1.0, jnp.where(sub == 4, norm, 0.0)))
            high, middle, low = pieces(rows)
            stacked = jnp.concatenate(
                [
                    jnp.where(sub < 5, high, pltpu.roll(low, 5, 0)),
                    jnp.where(sub < 4, high, jnp.where(sub == 4, low, pltpu.roll(high, 5, 0))),
                    jnp.where(sub == 3, 1.0, jnp.where(sub < 5, middle, 0.0)),
                    jnp.where(sub < 3, middle, 0.0),
                    jnp.zeros((128 - SPLIT_ROWS, 128), F32),
                ],
                axis=0,
            )
            tsplit[2 * pair + half] = stacked.T[:, 0:SPLIT_ROWS].astype(BF16)
        return carry

    lax.fori_loop(0, CAP // 2, prepare_target, 0)

    def prepare_sources(window, split, weights, at, lanes):
        split[3 * CAP, :, lanes] = jnp.zeros((SPLIT_ROWS, 128), BF16)
        weights[3 * CAP, at] = jnp.zeros((8, 128), F32)

        def one(pair, carry):
            tile = window[pl.ds(pl.multiple_of(8 * pair, 8), 8), :] - centre
            for half in range(2):
                base = tile if half == 0 else pltpu.roll(tile, 4, 0)
                norm = extended(base)
                rows = jnp.where(sub < 3, base, jnp.where(sub == 3, norm, jnp.where(sub == 4, 1.0, 0.0)))
                high, middle, low = pieces(rows)
                stacked = jnp.concatenate(
                    [
                        jnp.where(sub < 5, high, pltpu.roll(high, 5, 0)),
                        jnp.where(sub < 4, middle, jnp.where(sub == 4, 1.0, pltpu.roll(low, 5, 0))),
                        jnp.where(sub < 3, high, jnp.where(sub == 3, low, jnp.where(sub == 4, 1.0, 0.0))),
                        jnp.where(sub < 3, middle, 0.0),
                    ],
                    axis=0,
                )
                split[2 * pair + half, :, lanes] = stacked.astype(BF16)
                weights[2 * pair + half, at] = jnp.broadcast_to(base[3:4], (8, 128))
            return carry

        lax.fori_loop(0, 3 * CAP // 2, one, 0, unroll=2)

    for name in ("lskel", "ltrans", "bskel", "noise", "res", "sol"):
        loads[name].wait()
    skeleton_rows = padded_square(
        jnp.concatenate([lskel_ref[0], lskel_ref[1], lskel_ref[2]], axis=0) * SCALE
    ).T
    for row in range(3 * CAP):
        ftarget[row] = jnp.broadcast_to(skeleton_rows[0:64, row:row + 1], (64, 64))
    for component in range(3):
        farwin[component, CAP:2 * CAP, :] = lskel_ref[component] * SCALE
    farwin[:, 3 * CAP:, :] = jnp.zeros((4, 8, 64), F32)

    def near_slots(low, high, split, weights, width, first, slots, inline=False):
        chunks = [(k, j) for k in range(NEAR_NB) for j in range(width)]
        units = [chunks[i:i + 2] for i in range(0, len(chunks), 2)]

        def listed(slot, k):
            index = near_ref[k, slot]
            return jnp.where(index < 0, 3 * CAP, index)

        def buffer_of(u):
            return 0 if u == 0 else 1 + (u - 1) % 2

        def multiply(slot, u):
            parts = [split[listed(slot, k), :, 128 * j:128 * j + 128] for k, j in units[u]]
            sources = jnp.concatenate(parts, axis=1) if len(parts) > 1 else parts[0]
            products[buffer_of(u), :, 0:128 * len(parts)] = jnp.dot(
                tsplit[slot], sources, preferred_element_type=F32
            )

        def some_slots(step, carry):
            start = low + step * slots
            work = [(start + i, u) for i in range(slots) for u in range(len(units))]
            following = jnp.minimum(start + slots, CAP - 1)
            sums = []
            for at, (slot, u) in enumerate(work):
                if u == 0:
                    if first:
                        sums = [jnp.zeros((8, 128), F32)] * 16
                    else:
                        sums = [acc[slot, 8 * g:8 * g + 8, :] for g in range(16)]
                next_slot, next_u = work[at + 1] if at + 1 < len(work) else (following, 0)
                multiply(next_slot, next_u)
                weight = [weights[listed(slot, k), j] for k, j in units[u]]
                for g in range(16):
                    for i in range(len(weight)):
                        tile = decay(products[buffer_of(u), 8 * g:8 * g + 8, 128 * i:128 * i + 128])
                        sums[g] = sums[g] + tile * weight[i]
                if u + 1 == len(units):
                    if first:
                        for g in range(16):
                            acc[slot, 8 * g:8 * g + 8, :] = sums[g]
                    else:
                        whole = jnp.concatenate(sums, axis=0).T
                        near_rows[pl.ds(slot, 1), :] = jnp.sum(whole, axis=0, keepdims=True)
            return carry

        multiply(low, 0)
        if inline:
            some_slots(0, 0)
        else:
            lax.fori_loop(0, (high - low) // slots, some_slots, 0)

    for way in (1, -1):
        window_copies[way, 0].wait_recv()
    prepare_sources(win0, split0, wb0, 0, slice(0, 128))
    near_slots(0, 20, split0, wb0, 1, True, 4)

    for level in (2, 3, 4):
        @pl.when((core == 0) & (lax.rem(across, 2 ** (level - 1)) != 0))
        def _(level=level):
            send_to(
                psend.at[level - 1], pbuf.at[level - 1], p_s.at[0], p_r.at[level - 2], leaf, near
            ).wait_recv()

    @pl.when(core == 0)
    def _():
        relay.start()

    for copy in c_copies:
        copy.wait_recv()
    coeffs = cbuf[0] + cbuf[1] + cbuf[2] + cbuf[3]
    farwin[3, CAP:2 * CAP, :] = coeffs
    l_copies = []
    for number, (way, group) in enumerate(((1, 0), (-1, 2))):
        copy = send_to(
            farwin.at[:, pl.ds(CAP, CAP), :], farwin.at[:, pl.ds(CAP * group, CAP), :],
            l_s.at[number], l_r.at[number], leaf_at(way), near,
        )
        copy.start()
        l_copies.append(copy)

    total = jnp.zeros((64, 64), F32)
    for slot in range(CAP):
        total = total + ltrans_ref[slot] * farwin[3, CAP + slot:CAP + slot + 1, :]
    lifted = padded_square(jnp.broadcast_to(jnp.sum(total, axis=1, keepdims=True), (64, 128))).T[0:1, 0:64]

    @pl.when(core == 1)
    def _():
        relay.wait_recv()

    near_slots(20, CAP, split0, wb0, 1, True, 4, inline=True)
    bufa[place] = jnp.zeros((16, 128), F32)
    bufa[place, 0:1, 0:64] = lifted
    for level in range(LEVELS - 1):
        lifted = row_times(lifted, ancestor(level), True)
        bufa[place, level + 1:level + 2, 0:64] = lifted
    for component, (row, lane) in enumerate(((0, 64), (8, 0), (8, 64))):
        bufa[place, row:row + LEVELS, lane:lane + 64] = bskel_ref[component, :, 0, :] * SCALE

    def a_copy(step):
        return send_to(bufa.at[place], bufa.at[place], a_s.at[step], a_r.at[step], plane_peer(step), near)

    @pl.loop(1, PLANE)
    def _(step):
        a_copy(step).start()

    for way in (1, -1, 0):
        for step in range(1, NEAR):
            window_copies[way, step].wait_recv()
    for j in range(3):
        prepare_sources(wins[j + 1], split3, wb3, j, slice(128 * j, 128 * j + 128))
    near_slots(0, 6, split3, wb3, 3, False, 2)

    for copy in l_copies:
        copy.wait_recv()

    def one_far(slot, carry):
        target = [ftarget[c * CAP + slot] for c in range(3)]
        running = jnp.zeros((64, 64), F32)
        for k in range(2):
            index = far_ref[k, slot]
            index = jnp.where(index < 0, 3 * CAP, index)
            squared = jnp.zeros((64, 64), F32)
            for c in range(3):
                spacing = target[c] - farwin[c, pl.ds(index, 1), :]
                squared = squared + spacing * spacing
            running = running + decay(squared) * farwin[3, pl.ds(index, 1), :]
        return jnp.where(lanes64 == slot, jnp.sum(running, axis=1, keepdims=True), carry)

    near_slots(6, 10, split3, wb3, 3, False, 4, inline=True)
    far_columns = jnp.zeros((64, 128), F32)
    for slot in range(CAP):
        far_columns = one_far(slot, far_columns)
    fbuf[near] = padded_square(far_columns).T[0:CAP, 0:64] * AMPLITUDE
    f_copies = []
    for step in range(1, NEAR):
        copy = send_to(fbuf.at[near], fbuf.at[near], f_s.at[step - 1], f_r.at[step - 1], leaf, near_at(step))
        copy.start()
        f_copies.append(copy)


    @pl.loop(1, PLANE)
    def _(step):
        a_copy(step).wait_recv()

    low_lanes = lax.broadcasted_iota(jnp.int32, (1, 128), 1) < 64
    sums = [bufa[i, 0:8, :] for i in range(PLANE)]
    offset = 0
    for level in range(LEVELS):
        span = 2 ** min(level, 4)
        if 0 < level < 5:
            sums = [sums[2 * i] + sums[2 * i + 1] for i in range(len(sums) // 2)]
        for box in range(PLANE // span):
            own = bufa[box * span]
            rows = (
                jnp.where(low_lanes, sums[box][level:level + 1], own[level:level + 1]),
                own[8 + level:9 + level],
            )
            for half in range(2):
                if level < 3:
                    big[1, half, offset + box:offset + box + 1, :] = rows[half]
                else:
                    at = 4 * half + (0, 2, 3)[level - 3] + box
                    small[plane, at:at + 1, :] = rows[half]
        offset += PLANE // span

    def b_copy(step):
        return send_to(small.at[plane], small.at[plane], b_s.at[step], b_r.at[step], depth_peer(step), near)

    @pl.loop(1, PLANES)
    def _(step):
        b_copy(step).start()

    g_copies = []
    for number, (way, slot) in enumerate(((1, 0), (-1, 2))):
        copy = send_to(big.at[1], big.at[slot], g_s.at[number], g_r.at[number], depth_peer(way), near)
        copy.start()
        g_copies.append(copy)

    near_slots(10, 20, split3, wb3, 3, False, 2)

    @pl.loop(1, PLANES)
    def _(step):
        b_copy(step).wait_recv()

    for copy in g_copies:
        copy.wait_recv()
    near_slots(20, 22, split3, wb3, 3, False, 2, inline=True)
    targets[...] = jnp.zeros((128, 128), F32)
    for level in range(LEVELS):
        first = place // 2 ** level * 2 ** level
        for half in range(2):
            if level < 5:
                row = bufa[first, 8 * half + level:8 * half + level + 1, :]
            else:
                row = small[plane // 2 * 2, 4 * half + 3:4 * half + 4, :]
            targets[2 * level + half:2 * level + half + 1, :] = row
    turned = targets[...].T
    offsets = (0, 16, 24)
    field_columns = jnp.zeros((64, 128), F32)
    for level in range(LEVELS):
        box = leaf // 2 ** level
        boxes = PLANE * PLANES // 2 ** level
        target = [
            jnp.broadcast_to(turned[lane:lane + 64, 2 * level + half:2 * level + half + 1], (64, 64))
            for half, lane in ((0, 64), (1, 0), (1, 64))
        ]
        running = jnp.zeros((64, 64), F32)
        for away in (jnp.where(lax.rem(box, 2) == 1, -3, 3), -2, 2):
            other = box + away
            exists = (other >= 0) & (other < boxes)
            other = jnp.clip(other, 0, boxes - 1)
            if level < 3:
                each = PLANE // 2 ** level
                other_plane = other // each - plane + 1
                at = offsets[level] + lax.rem(other, each)
                halves = [big[other_plane, half, pl.ds(at, 1), :] for half in range(2)]
            elif level < 5:
                each = PLANE // 2 ** level
                at = (0, 2)[level - 3] + lax.rem(other, each)
                halves = [small[other // each, pl.ds(4 * half + at, 1), :] for half in range(2)]
            else:
                halves = [small[2 * other, 4 * half + 3:4 * half + 4, :] for half in range(2)]
                halves[0] = halves[0] + jnp.where(low_lanes, small[2 * other + 1, 3:4, :], 0.0)
            rows = [half[:, lane:lane + 64] for half in halves for lane in (0, 64)]
            squared = jnp.zeros((64, 64), F32)
            for c in range(3):
                spacing = target[c] - rows[c + 1]
                squared = squared + spacing * spacing
            running = running + decay(squared) * jnp.where(exists, rows[0], 0.0)
        field_columns = jnp.where(lanes64 == level, jnp.sum(running, axis=1, keepdims=True), field_columns)
    fields = padded_square(field_columns).T[0:8, 0:64] * AMPLITUDE
    downward = fields[LEVELS - 1:LEVELS]
    for level in range(LEVELS - 2, -1, -1):
        downward = fields[level:level + 1] + row_times(downward, ancestor(level), False)
    down_column = jnp.broadcast_to(
        jnp.concatenate([downward, jnp.zeros((1, 64), F32)], axis=1), (128, 128)
    ).T[0:64, 0:64]
    for slot in range(CAP):
        far_rows[slot:slot + 1, :] = jnp.sum(ltrans_ref[slot] * down_column, axis=0, keepdims=True)


    for copy in f_copies:
        copy.wait_recv()
    near_slots(22, CAP, split3, wb3, 3, False, 2, inline=True)
    expansion = far_rows[...] + (fbuf[0] + fbuf[1] + fbuf[2] + fbuf[3])
    expansion_columns = padded_square(expansion).T
    for slot in range(CAP):
        far_vals[slot:slot + 1, :] = jnp.sum(
            basis_ref[slot] * expansion_columns[0:64, slot:slot + 1], axis=0, keepdims=True
        )

    residual = jnp.where(occupied, res_ref[...], 0.0)
    image = jnp.where(
        occupied, noise_ref[...] * direction + AMPLITUDE * near_rows[...] + far_vals[...], 0.0
    )
    tile = jnp.zeros((8, 128), F32)
    for number, product in enumerate(
        (residual * residual, direction * image, residual * image, image * image)
    ):
        tile = jnp.where(sub == number, jnp.sum(product, axis=0, keepdims=True), tile)

    lane_group = lax.broadcasted_iota(jnp.int32, (8, 128), 1) // 32
    tile = tile + pltpu.roll(tile, 64, 1)
    tile = tile + pltpu.roll(tile, 32, 1)
    row = jnp.sum(jnp.where(sub == lane_group, tile, 0.0), axis=0, keepdims=True)

    mine = plane * NEAR + near
    hop1[mine] = row
    hop_copies = []
    peers = [(depth, step) for depth in range(PLANES) for step in range(NEAR) if depth or step]
    for depth, step in sorted(peers, key=lambda p: -min(p[0], PLANES - p[0]) - min(p[1], NEAR - p[1])):
        at = depth * NEAR + step
        copy = send_to(
            hop1.at[mine], hop1.at[mine], h1_s.at[at], h1_r.at[at], depth_peer(depth), near_at(step)
        )
        copy.start()
        hop_copies.append(copy)
    for copy in window_copies.values():
        copy.wait_send()

    @pl.when(core == 0)
    def _():
        relay.wait_send()
        for level in (2, 3, 4):
            @pl.when(lax.rem(across, 2 ** (level - 1)) == 0)
            def _(level=level):
                for span, copy in pair_copies:
                    if span == 2 ** (level - 1):
                        copy.wait_send()

    for copy in c_copies + l_copies + g_copies + f_copies:
        copy.wait_send()

    @pl.loop(1, PLANE)
    def _(step):
        a_copy(step).wait_send()

    @pl.loop(1, PLANES)
    def _(step):
        b_copy(step).wait_send()
    for copy in hop_copies:
        copy.wait_recv()
    hop2[place] = jnp.sum(hop1[...], axis=0)
    last_copies = []
    for step in sorted(range(1, PLANE), key=lambda p: -min(p, PLANE - p)):
        copy = send_to(
            hop2.at[place], hop2.at[place], h2_s.at[step], h2_r.at[step], plane_peer(step), near
        )
        copy.start()
        last_copies.append(copy)
    for copy in last_copies:
        copy.wait_recv()
    row = jnp.sum(hop2[...], axis=0)
    totals = jnp.sum(jnp.where(sub == lane_group, row, 0.0), axis=1, keepdims=True)
    norm_old, curvature, mixed, image_norm = (totals[i:i + 1] for i in range(4))
    step_length = norm_old / curvature
    norm_new = norm_old - 2.0 * step_length * mixed + step_length * step_length * image_norm
    new_residual = residual - step_length * image
    result_ref[0] = jnp.where(occupied, sol_ref[...], 0.0) + step_length * direction
    result_ref[1] = new_residual
    result_ref[2] = new_residual + norm_new / norm_old * direction

    for copy in hop_copies + last_copies:
        copy.wait_send()


def per_device(
    positions, noise_variance, solution, residual, direction, leaf_basis, leaf_skeleton,
    leaf_transfer, box_transfer, box_skeleton, leaf_count, near_list, far_list,
):
    vmem = pl.BlockSpec(memory_space=pltpu.VMEM)
    smem = pl.BlockSpec(memory_space=pltpu.SMEM)
    hbm = pl.BlockSpec(memory_space=pltpu.HBM)
    dma = pltpu.SemaphoreType.DMA
    slots = 3 * CAP + 1
    arrays = (
        positions, noise_variance, solution, residual, direction, leaf_basis, leaf_skeleton,
        leaf_transfer, box_transfer, box_skeleton.transpose(0, 2, 1, 3),
    )
    result = pl.pallas_call(
        kernel,
        out_shape=jax.ShapeDtypeStruct((3, CAP, 128), F32),
        in_specs=[smem] * 3 + [hbm] * len(arrays),
        out_specs=vmem,
        scratch_shapes=[
            *[pltpu.VMEM(array.shape, F32) for array in arrays],
            dma((len(arrays),)),
            *[pltpu.VMEM((12 * CAP, 128), F32)] * 4,
            pltpu.VMEM((slots, SPLIT_ROWS, 128), BF16),
            pltpu.VMEM((slots, SPLIT_ROWS, 384), BF16),
            pltpu.VMEM((slots, 1, 8, 128), F32),
            pltpu.VMEM((slots, 3, 8, 128), F32),
            pltpu.VMEM((CAP, 128, SPLIT_ROWS), BF16),
            pltpu.VMEM((3, 128, 256), F32),
            pltpu.VMEM((CAP, 128, 128), F32),
            pltpu.VMEM((CAP, 128), F32),
            pltpu.VMEM((NEAR, CAP, 64), F32),
            pltpu.VMEM((NEAR, CAP, 64), F32),
            pltpu.VMEM((4, 3 * CAP + 8, 64), F32),
            pltpu.VMEM((3 * CAP, 64, 64), F32),
            pltpu.VMEM((4, 32, 128), F32),
            pltpu.VMEM((4, 32, 128), F32),
            pltpu.VMEM((PLANE, 16, 128), F32),
            pltpu.VMEM((3, 2, 32, 128), F32),
            pltpu.VMEM((PLANES, 8, 128), F32),
            pltpu.VMEM((CAP, 64), F32),
            pltpu.VMEM((CAP, 64), F32),
            pltpu.VMEM((CAP, 128), F32),
            pltpu.VMEM((128, 128), F32),
            pltpu.VMEM((NEAR * PLANES, 1, 128), F32),
            pltpu.VMEM((PLANE, 1, 128), F32),
            dma((11,)), dma((11,)), dma((3,)), dma((3,)), dma((2,)), dma((2,)),
            dma((11,)), dma((3,)), dma, dma, dma((PLANE,)), dma((PLANE,)),
            dma((PLANES,)), dma((PLANES,)), dma((2,)), dma((2,)),
            dma((3,)), dma((3,)), dma((NEAR * PLANES,)), dma((NEAR * PLANES,)),
            dma((PLANE,)), dma((PLANE,)),
        ],
        compiler_params=pltpu.CompilerParams(
            collective_id=0, has_side_effects=True, vmem_limit_bytes=64 * 2**20
        ),
        name="iteration",
    )(leaf_count, near_list.T, far_list.T, *arrays)
    return result[0], result[1], result[2]


def solution(mesh):
    return jax.shard_map(
        per_device,
        mesh=mesh,
        in_specs=(
            P(None, "leaf", "near"),
            P("leaf", "near"),
            P("leaf", "near"),
            P("leaf", "near"),
            P("leaf", "near"),
            P("leaf", None, "near"),
            P(None, "leaf", None),
            P("leaf", None, None),
            P("leaf", None, None, None),
            P(None, "leaf", None, None),
            P("leaf"),
            P("leaf", None),
            P("leaf", "near"),
        ),
        out_specs=(P("leaf", "near"), P("leaf", "near"), P("leaf", "near")),
        check_vma=False,
    )
```
